32 devices in a mesh: lag: 4 (over y, x), row: 8 (over z, core).
Axes of the slice: x: 2, y: 2, z: 4, core: 2. Of those that a mesh axis runs over, the one named last changes fastest.
Arguments:
- newest: bfloat16 [512, 8192], P('lag', 'row'), may hold values from -6 to 6
- earlier: bfloat16 [3, 8192], P(None, 'row'), may hold values from -6 to 6
- lag_matrices: bfloat16 [4, 8192, 8192], P('lag', 'row'), may hold values from -0.03125 to 0.03125
Outputs:
- forces: float32 [512, 8192], P('lag', 'row')
The draws below stay inside these ranges and needn't reach their ends.
All inputs are finite; a program needn't handle non-finite values.
Results may differ from the reference program's by a relative error of at most 0.0003.
Values may be sent and summed in bfloat16 or wider, within the bound.
A program may use at most 64 MiB of HBM per device.

```python
import jax
import jax.numpy as jnp
from jax import lax

DOF = 8192
STEPS = 512
LAGS = 4


def level_of(key, extent, shards, least, high):
    def one(position, shards_of):
        heights = jax.random.uniform(jax.random.fold_in(jax.random.fold_in(key, 6), position), (shards_of,), jnp.float32, least / len(shards), high / len(shards))
        return jnp.repeat(jnp.exp(heights), extent[position] // shards_of).reshape((-1,) + (1,) * (len(extent) - position - 1))

    level = one(*shards[0])
    for cut in shards[1:]:
        level = level * one(*cut)
    return level


def bell_draw(stream_key, extent, scale, bound, shards=(), held_as=jnp.bfloat16):
    drawn = jax.random.normal(stream_key, extent, jnp.float32) * scale
    if len(shards) > 0:
        drawn = level_of(stream_key, extent, shards, -0.22, 0.18) * drawn
    return jnp.clip(drawn, min=-bound, max=bound).astype(held_as)


def setup_inputs(seed: int = 0) -> dict:
    arg_keys = jax.random.split(jax.random.key(seed), 4)
    newest = bell_draw(arg_keys[0], (STEPS, DOF), 1.0, 6.0, ((0, 4), (1, 8)))
    earlier = bell_draw(arg_keys[1], (LAGS - 1, DOF), 1.0, 6.0, ((1, 8),))
    lag_matrices = bell_draw(arg_keys[2], (LAGS, DOF, DOF), (DOF * LAGS) ** -0.5, 0.03125, ((0, 4), (1, 8)))
    return dict(newest=newest, earlier=earlier, lag_matrices=lag_matrices)


def reference(newest, earlier, lag_matrices):
    record = jnp.concatenate([earlier, newest], axis=0)

    def add_lag(total, inputs):
        lag_number, matrix = inputs
        offset = (LAGS - 1 - lag_number).astype(jnp.int32)
        window = lax.dynamic_slice_in_dim(record, offset, STEPS, 0)
        return total + jnp.dot(window, matrix.T, preferred_element_type=jnp.float32), None

    zeros = jnp.zeros((STEPS, DOF), jnp.float32)
    lag_numbers = jnp.arange(LAGS).astype(jnp.int32)
    forces, unused = lax.scan(add_lag, zeros, (lag_numbers, lag_matrices))
    return forces
```

```python
import jax
import jax.numpy as jnp
from jax import lax
from jax.experimental import pallas as pl
from jax.experimental.pallas import tpu as pltpu
from jax.sharding import PartitionSpec as P

MESH = pl.DeviceIdType.MESH
PAD = 16
NZ = 4


def product(window, matrix):
    return lax.dot_general(
        window, matrix, (((1,), (1,)), ((), ())), preferred_element_type=jnp.float32
    )


def on_device_general(newest, earlier, lag_matrices):
    lag_index = lax.axis_index("lag")
    matrix = lag_matrices[0]
    own_steps = newest.shape[0]
    earlier_rows = earlier.shape[0]
    wide_newest, wide_earlier = (
        lax.all_gather(newest, "row", axis=1, tiled=True),
        lax.all_gather(earlier, "row", axis=1, tiled=True),
    )
    history = lax.all_gather(wide_newest, "lag", axis=0, tiled=True)
    record = jnp.concatenate([wide_earlier, history], axis=0)
    window = lax.dynamic_slice_in_dim(
        record, jnp.int32(0) + earlier_rows - lag_index, own_steps * lax.axis_size("lag"), 0
    )
    return lax.psum_scatter(product(window, matrix), "lag", scatter_dimension=0, tiled=True)


def kernel(new_ref, ear_ref, mat_ref, out_ref,
           mat, hist, ebuf, acc, s_d, s_x, s_y, r_d, r_1, r_2,
           loc, zs, zr, xs, xr, ys, yr, ss, sr, es, er, fs, fr):
    lag, row = lax.axis_index("lag"), lax.axis_index("row")
    x, y = lag % 2, lag // 2
    z, core = row // 2, row % 2
    sib = row + 1 - 2 * core
    t0, tx, ty = lag, 2 * y + 1 - x, 2 * (1 - y) + x
    td = 2 * (1 - y) + 1 - x
    steps, width = new_ref.shape
    half = steps // 2
    x_dev, y_dev = {"lag": tx, "row": row}, {"lag": ty, "row": row}
    sib_dev = {"lag": lag, "row": sib}

    mat_copy = pltpu.make_async_copy(mat_ref.at[0], mat, loc.at[0])
    mat_copy.start()

    def rows(t, h, n):
        return pl.ds(pl.multiple_of(PAD + t * steps + h * half, 16), n)

    own_copy = pltpu.make_async_copy(new_ref, hist.at[row, rows(t0, 0, steps)], loc.at[1])
    own_copy.start()
    own_e = pltpu.make_async_copy(ear_ref, ebuf.at[row], loc.at[2])
    own_e.start()

    barrier = pltpu.get_barrier_semaphore()
    for dev in (x_dev, y_dev):
        pl.semaphore_signal(barrier, inc=1, device_id=dev, device_id_type=MESH)
    for j in range(1, 2 * NZ):
        pl.semaphore_signal(barrier, inc=1, device_id={"lag": lag, "row": (row + j) % (2 * NZ)},
                            device_id_type=MESH)
    pl.semaphore_wait(barrier, 2 * NZ + 1)

    def copy(src, dst, ssem, rsem, dev):
        return pltpu.make_async_remote_copy(
            src_ref=src, dst_ref=dst, send_sem=ssem, recv_sem=rsem, device_id=dev,
            device_id_type=MESH)

    def place(r, t, h, n):
        return hist.at[r, rows(t, h, n)]

    z_kind = ((t0, 0, steps), (tx, 0, half), (ty, 1, half))
    x_kind = ((t0, 0, half), (t0, 1, half), (ty, 1, half))
    y_kind = ((t0, 1, half), (t0, 0, half), (tx, 0, half))
    s_kind = tuple((t, 0, steps) for t in (t0, tx, ty, td))
    x_got = ((tx, 0, half), (tx, 1, half), (td, 1, half))
    y_got = ((ty, 1, half), (ty, 0, half), (td, 0, half))

    def fam(zz):
        return 2 * zz + core

    def z_msg(up, zz, m):
        dev = {"lag": lag, "row": row + 2 if up else row - 2}
        ref = place(fam(zz), *z_kind[m])
        return copy(ref, ref, zs.at[int(up), zz, m], zr.at[zz, m], dev)

    def z_own(up):
        dev = {"lag": lag, "row": row + 2 if up else row - 2}
        return copy(new_ref, place(row, *z_kind[0]), zs.at[int(up), z, 0], zr.at[z, 0], dev)

    def x_msg(zz, m):
        ref = place(fam(zz), *x_kind[m])
        return copy(ref, ref, xs.at[zz, m], xr.at[zz, m], x_dev)

    def y_msg(zz, m):
        ref = place(fam(zz), *y_kind[m])
        return copy(ref, ref, ys.at[zz, m], yr.at[zz, m], y_dev)

    def s_msg(zz, m):
        ref = place(fam(zz), *s_kind[m])
        return copy(ref, ref, ss.at[zz, m], sr.at[zz, m], sib_dev)

    def z_wait(zz, m):
        ref = place(fam(zz), *z_kind[m])
        copy(ref, ref, zs.at[0, zz, m], zr.at[zz, m], x_dev).wait_recv()

    def x_wait(zz, m):
        ref = place(fam(zz), *x_got[m])
        copy(ref, ref, xs.at[zz, m], xr.at[zz, m], x_dev).wait_recv()

    def y_wait(zz, m):
        ref = place(fam(zz), *y_got[m])
        copy(ref, ref, ys.at[zz, m], yr.at[zz, m], y_dev).wait_recv()

    def s_wait(zz, m):
        ref = place(2 * zz + 1 - core, *s_kind[m])
        copy(ref, ref, ss.at[zz, m], sr.at[zz, m], sib_dev).wait_recv()

    can_up, can_down = z < NZ - 1, z > 0

    def own_half(h):
        return new_ref.at[pl.ds(h * half, half)]

    @pl.when(can_up)
    def _():
        z_own(True).start()

    @pl.when(can_down)
    def _():
        z_own(False).start()

    own_x = [copy(own_half(h), place(row, t0, h, half), xs.at[z, h], xr.at[z, h], x_dev)
             for h in (0, 1)]
    own_y = [copy(own_half(1 - m), place(row, t0, 1 - m, half), ys.at[z, m], yr.at[z, m], y_dev)
             for m in (0, 1)]
    for m in (0, 1):
        own_x[m].start()
        own_y[m].start()
    copy(new_ref, place(row, t0, 0, steps), ss.at[z, 0], sr.at[z, 0], sib_dev).start()

    def e_msg(j):
        to = (row + j) % (2 * NZ)
        return copy(ear_ref, ebuf.at[row], es.at[j], er.at[row], {"lag": lag, "row": to})

    def e_wait(j):
        frm = (row + j) % (2 * NZ)
        copy(ear_ref, ebuf.at[frm], es.at[j], er.at[frm], sib_dev).wait_recv()

    for j in range(1, 2 * NZ):
        e_msg(j).start()

    def z_on_both(m):
        @pl.when(can_up)
        def _():
            z_msg(True, z, m).start()

        @pl.when(can_down)
        def _():
            z_msg(False, z, m).start()

    def arrive(zz, m, up):
        z_wait(zz, m)

        @pl.when(can_up if up else can_down)
        def _():
            z_msg(up, zz, m).start()

        if m == 0:
            x_msg(zz, 1).start()
            y_msg(zz, 1).start()
            s_msg(zz, 0).start()
        elif m == 1:
            y_msg(zz, 2).start()
        else:
            x_msg(zz, 2).start()

    def both(d, act):
        @pl.when(z >= d)
        def _():
            act(z - d, True)

        @pl.when(z + d < NZ)
        def _():
            act(z + d, False)

    def rest(zz):
        x_wait(zz, 1)
        s_msg(zz, 1).start()
        y_wait(zz, 1)
        s_msg(zz, 2).start()
        x_wait(zz, 2)
        y_wait(zz, 2)
        s_msg(zz, 3).start()

    tile = 256

    def compute(zz, first=False):
        for m in range(4):
            s_wait(zz, m)

        def body(i, carry):
            n = pl.ds(pl.multiple_of(i * tile, tile), tile)
            total = None
            for c in range(2):
                r = 2 * zz + c
                cols = pl.ds(pl.multiple_of(r * width, width), width)
                term = product(hist[r], mat[n, cols])
                total = term if total is None else total + term
            if first:
                acc[:, n] = total
            else:
                acc[:, n] += total
            return carry

        lax.fori_loop(0, acc.shape[1] // tile, body, 0)

    x_wait(z, 0)
    z_on_both(1)
    y_msg(z, 2).start()
    y_wait(z, 0)
    z_on_both(2)
    x_msg(z, 2).start()
    both(1, lambda zz, up: arrive(zz, 0, up))
    own_copy.wait()
    own_e.wait()
    rest(z)
    for m in (1, 2):
        both(1, lambda zz, up: arrive(zz, m, up))
    for j in range(1, 2 * NZ):
        e_wait(j)
    chunk = ear_ref.shape[1]
    for r in range(2 * NZ):
        e = ebuf[r].astype(jnp.float32)
        for j in range(width // chunk):
            cut = 4 * j + 4
            piece = e if cut == PAD else jnp.concatenate([e[cut:], e[:cut]], axis=0)
            hist[r, 0:PAD, j * chunk:(j + 1) * chunk] = piece.astype(hist.dtype)
    mat_copy.wait()
    compute(z, first=True)
    for d in (2, 3):
        both(d, lambda zz, up: arrive(zz, 0, up))
        both(d - 1, lambda zz, up: rest(zz))
        if d == 2:
            for m in (1, 2):
                both(d, lambda zz, up: arrive(zz, m, up))
            both(1, lambda zz, up: compute(zz))
        else:
            for m in (1, 2):
                both(d, lambda zz, up: arrive(zz, m, up))
            both(2, lambda zz, up: compute(zz))
    both(3, lambda zz, up: rest(zz))
    both(3, lambda zz, up: compute(zz))

    def shifted(t, h, n0):
        start = pl.multiple_of(PAD - 8 + t * steps + h * half, 8)
        part = acc[pl.ds(start, half + 8), n0:n0 + tile]
        got = part[8:]
        for k in range(1, 4):
            got = jnp.where(lag == k, part[8 - k:8 - k + half], got)
        return got

    def fill(dst, t, h):
        for n0 in range(0, width, tile):
            dst[h * half:(h + 1) * half, n0:n0 + tile] = shifted(t, h, n0)

    def f_msg(src, dst, h, i, dev):
        cut = pl.ds(h * half, half)
        return copy(src.at[cut], dst.at[cut], fs.at[i], fr.at[i], dev)

    hop_y, hop_x = f_msg(s_d, r_d, 0, 0, y_dev), f_msg(s_d, r_d, 1, 1, x_dev)
    dir_x, dir_y = f_msg(s_x, r_1, 1, 2, x_dev), f_msg(s_y, r_1, 0, 3, y_dev)
    last_x, last_y = f_msg(s_x, r_2, 0, 4, x_dev), f_msg(s_y, r_2, 1, 5, y_dev)
    fill(s_d, td, 0)
    hop_y.start()
    fill(s_d, td, 1)
    hop_x.start()
    fill(s_x, tx, 1)
    dir_x.start()
    fill(s_y, ty, 0)
    dir_y.start()
    fill(s_x, tx, 0)
    fill(s_y, ty, 1)
    hop_y.wait_recv()
    s_x[0:half] += r_d[0:half]
    last_x.start()
    hop_x.wait_recv()
    s_y[half:steps] += r_d[half:steps]
    last_y.start()
    fill(out_ref, t0, 0)
    fill(out_ref, t0, 1)
    dir_x.wait_recv()
    dir_y.wait_recv()
    out_ref[...] += r_1[...]
    last_x.wait_recv()
    out_ref[0:half] += r_2[0:half]
    last_y.wait_recv()
    out_ref[half:steps] += r_2[half:steps]

    for c in (hop_y, hop_x, dir_x, dir_y, last_x, last_y):
        c.wait_send()
    for j in range(1, 2 * NZ):
        e_msg(j).wait_send()
    x_msg(z, 0).wait_send()
    y_msg(z, 0).wait_send()
    for zz in range(NZ):
        for m in range(3):
            @pl.when(can_up & (z >= zz))
            def _():
                z_msg(True, zz, m).wait_send()

            @pl.when(can_down & (z <= zz))
            def _():
                z_msg(False, zz, m).wait_send()
        for m in (1, 2):
            x_msg(zz, m).wait_send()
            y_msg(zz, m).wait_send()
        for m in range(4):
            s_msg(zz, m).wait_send()


def on_device(newest, earlier, lag_matrices):
    steps, width = newest.shape
    height = lag_matrices.shape[1]
    count = earlier.shape[0]
    groups = PAD // 4
    packed = jnp.pad(earlier, ((4 - count, 0), (0, 0)))
    packed = packed.reshape(4, groups, width // groups).transpose(1, 0, 2).reshape(PAD, width // groups)
    any_spec = pl.BlockSpec(memory_space=pl.ANY)
    vmem = pl.BlockSpec(memory_space=pltpu.VMEM)
    dma = pltpu.SemaphoreType.DMA
    block = pltpu.VMEM((steps, height), jnp.float32)
    return pl.pallas_call(
        kernel,
        out_shape=jax.ShapeDtypeStruct((steps, height), jnp.float32),
        in_specs=[any_spec, any_spec, any_spec],
        out_specs=vmem,
        scratch_shapes=[
            pltpu.VMEM((height, 2 * NZ * width), jnp.bfloat16),
            pltpu.VMEM((2 * NZ, PAD + 4 * steps, width), jnp.bfloat16),
            pltpu.VMEM((2 * NZ, PAD, width // groups), jnp.bfloat16),
            pltpu.VMEM((PAD + 4 * steps, height), jnp.float32),
            block, block, block, block, block, block,
            dma((3,)),
            dma((2, NZ, 3)), dma((NZ, 3)),
            dma((NZ, 3)), dma((NZ, 3)),
            dma((NZ, 3)), dma((NZ, 3)),
            dma((NZ, 4)), dma((NZ, 4)),
            dma((2 * NZ,)), dma((2 * NZ,)),
            dma((6,)), dma((6,)),
        ],
        compiler_params=pltpu.CompilerParams(
            collective_id=0, has_side_effects=True, vmem_limit_bytes=48 * 1024 * 1024
        ),
        cost_estimate=pl.CostEstimate(
            flops=2 * 4 * steps * height * 2 * NZ * width,
            bytes_accessed=height * 2 * NZ * width * 2, transcendentals=0),
    )(newest, packed, lag_matrices)


def solution(mesh):
    in_specs = (P("lag", "row"), P(None, "row"), P("lag", "row", None))
    out_specs = P("lag", "row")
    fits = mesh.shape["lag"] == 4 and mesh.shape["row"] == 2 * NZ
    return jax.shard_map(
        on_device if fits else on_device_general,
        mesh=mesh, in_specs=in_specs, out_specs=out_specs, check_vma=False
    )
```

```python
import jax
import jax.numpy as jnp
from jax import lax
from jax.experimental import pallas as pl
from jax.experimental.pallas import tpu as pltpu
from jax.sharding import PartitionSpec as P

MESH = pl.DeviceIdType.MESH
PAD = 16
NZ = 4


def product(window, matrix):
    return lax.dot_general(
        window, matrix, (((1,), (1,)), ((), ())), preferred_element_type=jnp.float32
    )


def on_device_general(newest, earlier, lag_matrices):
    lag_index = lax.axis_index("lag")
    matrix = lag_matrices[0]
    own_steps = newest.shape[0]
    earlier_rows = earlier.shape[0]
    wide_newest, wide_earlier = (
        lax.all_gather(newest, "row", axis=1, tiled=True),
        lax.all_gather(earlier, "row", axis=1, tiled=True),
    )
    history = lax.all_gather(wide_newest, "lag", axis=0, tiled=True)
    record = jnp.concatenate([wide_earlier, history], axis=0)
    window = lax.dynamic_slice_in_dim(
        record, jnp.int32(0) + earlier_rows - lag_index, own_steps * lax.axis_size("lag"), 0
    )
    return lax.psum_scatter(product(window, matrix), "lag", scatter_dimension=0, tiled=True)


def kernel(new_ref, ear_ref, mat_ref, out_ref,
           mat, hist, ebuf, acc, s_d, s_x, s_y, r_d, r_1, r_2,
           loc, zs, zr, xs, xr, ys, yr, ss, sr, es, er, fs, fr):
    lag, row = lax.axis_index("lag"), lax.axis_index("row")
    x, y = lag % 2, lag // 2
    z, core = row // 2, row % 2
    sib = row + 1 - 2 * core
    t0, tx, ty = lag, 2 * y + 1 - x, 2 * (1 - y) + x
    td = 2 * (1 - y) + 1 - x
    steps, width = new_ref.shape
    half = steps // 2
    x_dev, y_dev = {"lag": tx, "row": row}, {"lag": ty, "row": row}
    sib_dev = {"lag": lag, "row": sib}

    mat_copy = pltpu.make_async_copy(mat_ref.at[0], mat, loc.at[0])
    mat_copy.start()

    def rows(t, h, n):
        return pl.ds(pl.multiple_of(PAD + t * steps + h * half, 16), n)

    own_copy = pltpu.make_async_copy(new_ref, hist.at[row, rows(t0, 0, steps)], loc.at[1])
    own_copy.start()
    own_e = pltpu.make_async_copy(ear_ref, ebuf.at[row], loc.at[2])
    own_e.start()

    barrier = pltpu.get_barrier_semaphore()
    for dev in (x_dev, y_dev):
        pl.semaphore_signal(barrier, inc=1, device_id=dev, device_id_type=MESH)
    for j in range(1, 2 * NZ):
        pl.semaphore_signal(barrier, inc=1, device_id={"lag": lag, "row": (row + j) % (2 * NZ)},
                            device_id_type=MESH)
    pl.semaphore_wait(barrier, 2 * NZ + 1)

    def copy(src, dst, ssem, rsem, dev):
        return pltpu.make_async_remote_copy(
            src_ref=src, dst_ref=dst, send_sem=ssem, recv_sem=rsem, device_id=dev,
            device_id_type=MESH)

    def place(r, t, h, n):
        return hist.at[r, rows(t, h, n)]

    z_kind = ((t0, 0, steps), (tx, 0, half), (ty, 1, half))
    x_kind = ((t0, 0, half), (t0, 1, half), (ty, 1, half))
    y_kind = ((t0, 1, half), (t0, 0, half), (tx, 0, half))
    s_kind = tuple((t, 0, steps) for t in (t0, tx, ty, td))
    x_got = ((tx, 0, half), (tx, 1, half), (td, 1, half))
    y_got = ((ty, 1, half), (ty, 0, half), (td, 0, half))

    def fam(zz):
        return 2 * zz + core

    def z_msg(up, zz, m):
        dev = {"lag": lag, "row": row + 2 if up else row - 2}
        ref = place(fam(zz), *z_kind[m])
        return copy(ref, ref, zs.at[int(up), zz, m], zr.at[zz, m], dev)

    def z_own(up):
        dev = {"lag": lag, "row": row + 2 if up else row - 2}
        return copy(new_ref, place(row, *z_kind[0]), zs.at[int(up), z, 0], zr.at[z, 0], dev)

    def x_msg(zz, m):
        ref = place(fam(zz), *x_kind[m])
        return copy(ref, ref, xs.at[zz, m], xr.at[zz, m], x_dev)

    def y_msg(zz, m):
        ref = place(fam(zz), *y_kind[m])
        return copy(ref, ref, ys.at[zz, m], yr.at[zz, m], y_dev)

    def s_msg(zz, m):
        ref = place(fam(zz), *s_kind[m])
        return copy(ref, ref, ss.at[zz, m], sr.at[zz, m], sib_dev)

    def z_wait(zz, m):
        ref = place(fam(zz), *z_kind[m])
        copy(ref, ref, zs.at[0, zz, m], zr.at[zz, m], x_dev).wait_recv()

    def x_wait(zz, m):
        ref = place(fam(zz), *x_got[m])
        copy(ref, ref, xs.at[zz, m], xr.at[zz, m], x_dev).wait_recv()

    def y_wait(zz, m):
        ref = place(fam(zz), *y_got[m])
        copy(ref, ref, ys.at[zz, m], yr.at[zz, m], y_dev).wait_recv()

    def s_wait(zz, m):
        ref = place(2 * zz + 1 - core, *s_kind[m])
        copy(ref, ref, ss.at[zz, m], sr.at[zz, m], sib_dev).wait_recv()

    can_up, can_down = z < NZ - 1, z > 0

    def own_half(h):
        return new_ref.at[pl.ds(h * half, half)]

    @pl.when(can_up)
    def _():
        z_own(True).start()

    @pl.when(can_down)
    def _():
        z_own(False).start()

    own_x = [copy(own_half(h), place(row, t0, h, half), xs.at[z, h], xr.at[z, h], x_dev)
             for h in (0, 1)]
    own_y = [copy(own_half(1 - m), place(row, t0, 1 - m, half), ys.at[z, m], yr.at[z, m], y_dev)
             for m in (0, 1)]
    for m in (0, 1):
        own_x[m].start()
        own_y[m].start()
    copy(new_ref, place(row, t0, 0, steps), ss.at[z, 0], sr.at[z, 0], sib_dev).start()

    def e_msg(j):
        to = (row + j) % (2 * NZ)
        return copy(ear_ref, ebuf.at[row], es.at[j], er.at[row], {"lag": lag, "row": to})

    def e_wait(j):
        frm = (row + j) % (2 * NZ)
        copy(ear_ref, ebuf.at[frm], es.at[j], er.at[frm], sib_dev).wait_recv()

    for j in range(1, 2 * NZ):
        e_msg(j).start()

    wide_up, wide_down = z < NZ - 2, z > 1
    at_end = (z == 0) | (z == NZ - 1)

    def z_on_both(m):
        @pl.when(wide_up)
        def _():
            z_msg(True, z, m).start()

        @pl.when(wide_down)
        def _():
            z_msg(False, z, m).start()

    def arrive(zz, m, up):
        z_wait(zz, m)

        @pl.when(can_up if up else can_down)
        def _():
            z_msg(up, zz, m).start()

        if m == 0:
            x_msg(zz, 1).start()
            y_msg(zz, 1).start()
            s_msg(zz, 0).start()
        elif m == 1:
            y_msg(zz, 2).start()
        else:
            x_msg(zz, 2).start()

    def both(d, act):
        @pl.when(z >= d)
        def _():
            act(z - d, True)

        @pl.when(z + d < NZ)
        def _():
            act(z + d, False)

    def rest(zz):
        x_wait(zz, 1)
        s_msg(zz, 1).start()
        y_wait(zz, 1)
        s_msg(zz, 2).start()
        x_wait(zz, 2)
        y_wait(zz, 2)
        s_msg(zz, 3).start()

    tile = 512

    def compute(zz, first=False):
        for m in range(4):
            s_wait(zz, m)

        def body(i, carry):
            n = pl.ds(pl.multiple_of(i * tile, tile), tile)
            total = None
            for c in range(2):
                r = 2 * zz + c
                cols = pl.ds(pl.multiple_of(r * width, width), width)
                term = product(hist[r], mat[n, cols])
                total = term if total is None else total + term
            if first:
                acc[:, n] = total
            else:
                acc[:, n] += total
            return carry

        lax.fori_loop(0, acc.shape[1] // tile, body, 0)

    x_wait(z, 0)
    z_on_both(1)
    y_msg(z, 2).start()
    y_wait(z, 0)
    z_on_both(2)
    x_msg(z, 2).start()
    inner = jnp.where(z == 0, 1, NZ - 2)

    @pl.when(at_end)
    def _():
        z_wait(inner, 0)
        for m in (0, 1):
            x_msg(inner, m).start()
            y_msg(inner, m).start()
        s_msg(inner, 0).start()

    @pl.when(jnp.logical_not(at_end))
    def _():
        arrive(z - 1, 0, True)
        arrive(z + 1, 0, False)

    own_copy.wait()
    own_e.wait()
    rest(z)
    @pl.when(at_end)
    def _():
        x_wait(inner, 0)
        y_msg(inner, 2).start()
        y_wait(inner, 0)
        x_msg(inner, 2).start()

    @pl.when(jnp.logical_not(at_end))
    def _():
        for m in (1, 2):
            arrive(z - 1, m, True)
            arrive(z + 1, m, False)

    for j in range(1, 2 * NZ):
        e_wait(j)
    chunk = ear_ref.shape[1]
    for r in range(2 * NZ):
        e = ebuf[r].astype(jnp.float32)
        for j in range(width // chunk):
            cut = 4 * j + 4
            piece = e if cut == PAD else jnp.concatenate([e[cut:], e[:cut]], axis=0)
            hist[r, 0:PAD, j * chunk:(j + 1) * chunk] = piece.astype(hist.dtype)
    mat_copy.wait()
    compute(z, first=True)
    for d in (2, 3):
        both(d, lambda zz, up: arrive(zz, 0, up))
        both(d - 1, lambda zz, up: rest(zz))
        if d == 2:
            for m in (1, 2):
                both(d, lambda zz, up: arrive(zz, m, up))
            both(1, lambda zz, up: compute(zz))
        else:
            for m in (1, 2):
                both(d, lambda zz, up: arrive(zz, m, up))
            both(2, lambda zz, up: compute(zz))
    both(3, lambda zz, up: rest(zz))
    both(3, lambda zz, up: compute(zz))

    def shifted(t, h, n0):
        start = pl.multiple_of(PAD - 8 + t * steps + h * half, 8)
        part = acc[pl.ds(start, half + 8), n0:n0 + 256]
        got = part[8:]
        for k in range(1, 4):
            got = jnp.where(lag == k, part[8 - k:8 - k + half], got)
        return got

    def fill(dst, t, h):
        for n0 in range(0, width, 256):
            dst[h * half:(h + 1) * half, n0:n0 + 256] = shifted(t, h, n0)

    def f_msg(src, dst, h, i, dev):
        cut = pl.ds(h * half, half)
        return copy(src.at[cut], dst.at[cut], fs.at[i], fr.at[i], dev)

    hop_y, hop_x = f_msg(s_d, r_d, 0, 0, y_dev), f_msg(s_d, r_d, 1, 1, x_dev)
    dir_x, dir_y = f_msg(s_x, r_1, 1, 2, x_dev), f_msg(s_y, r_1, 0, 3, y_dev)
    last_x, last_y = f_msg(s_x, r_2, 0, 4, x_dev), f_msg(s_y, r_2, 1, 5, y_dev)
    fill(s_d, td, 0)
    hop_y.start()
    fill(s_d, td, 1)
    hop_x.start()
    fill(s_x, tx, 1)
    dir_x.start()
    fill(s_y, ty, 0)
    dir_y.start()
    fill(s_x, tx, 0)
    fill(s_y, ty, 1)
    hop_y.wait_recv()
    s_x[0:half] += r_d[0:half]
    last_x.start()
    hop_x.wait_recv()
    s_y[half:steps] += r_d[half:steps]
    last_y.start()
    fill(out_ref, t0, 0)
    fill(out_ref, t0, 1)
    dir_x.wait_recv()
    dir_y.wait_recv()
    out_ref[...] += r_1[...]
    last_x.wait_recv()
    out_ref[0:half] += r_2[0:half]
    last_y.wait_recv()
    out_ref[half:steps] += r_2[half:steps]

    for c in (hop_y, hop_x, dir_x, dir_y, last_x, last_y):
        c.wait_send()
    for j in range(1, 2 * NZ):
        e_msg(j).wait_send()
    x_msg(z, 0).wait_send()
    y_msg(z, 0).wait_send()

    @pl.when(at_end)
    def _():
        x_msg(inner, 0).wait_send()
        y_msg(inner, 0).wait_send()

    for zz in range(NZ):
        for m in range(3):
            @pl.when(can_up & (z >= zz) & ((z != zz) | wide_up | (m == 0)))
            def _():
                z_msg(True, zz, m).wait_send()

            @pl.when(can_down & (z <= zz) & ((z != zz) | wide_down | (m == 0)))
            def _():
                z_msg(False, zz, m).wait_send()
        for m in (1, 2):
            x_msg(zz, m).wait_send()
            y_msg(zz, m).wait_send()
        for m in range(4):
            s_msg(zz, m).wait_send()


def on_device(newest, earlier, lag_matrices):
    steps, width = newest.shape
    height = lag_matrices.shape[1]
    count = earlier.shape[0]
    groups = PAD // 4
    packed = jnp.pad(earlier, ((4 - count, 0), (0, 0)))
    packed = packed.reshape(4, groups, width // groups).transpose(1, 0, 2).reshape(PAD, width // groups)
    any_spec = pl.BlockSpec(memory_space=pl.ANY)
    vmem = pl.BlockSpec(memory_space=pltpu.VMEM)
    dma = pltpu.SemaphoreType.DMA
    block = pltpu.VMEM((steps, height), jnp.float32)
    return pl.pallas_call(
        kernel,
        out_shape=jax.ShapeDtypeStruct((steps, height), jnp.float32),
        in_specs=[any_spec, any_spec, any_spec],
        out_specs=vmem,
        scratch_shapes=[
            pltpu.VMEM((height, 2 * NZ * width), jnp.bfloat16),
            pltpu.VMEM((2 * NZ, PAD + 4 * steps, width), jnp.bfloat16),
            pltpu.VMEM((2 * NZ, PAD, width // groups), jnp.bfloat16),
            pltpu.VMEM((PAD + 4 * steps, height), jnp.float32),
            block, block, block, block, block, block,
            dma((3,)),
            dma((2, NZ, 3)), dma((NZ, 3)),
            dma((NZ, 3)), dma((NZ, 3)),
            dma((NZ, 3)), dma((NZ, 3)),
            dma((NZ, 4)), dma((NZ, 4)),
            dma((2 * NZ,)), dma((2 * NZ,)),
            dma((6,)), dma((6,)),
        ],
        compiler_params=pltpu.CompilerParams(
            collective_id=0, has_side_effects=True, vmem_limit_bytes=48 * 1024 * 1024
        ),
        cost_estimate=pl.CostEstimate(
            flops=2 * 4 * steps * height * 2 * NZ * width,
            bytes_accessed=height * 2 * NZ * width * 2, transcendentals=0),
    )(newest, packed, lag_matrices)


def solution(mesh):
    in_specs = (P("lag", "row"), P(None, "row"), P("lag", "row", None))
    out_specs = P("lag", "row")
    fits = mesh.shape["lag"] == 4 and mesh.shape["row"] == 2 * NZ
    return jax.shard_map(
        on_device if fits else on_device_general,
        mesh=mesh, in_specs=in_specs, out_specs=out_specs, check_vma=False
    )
```

```python
import jax
import jax.numpy as jnp
from jax import lax
from jax.experimental import pallas as pl
from jax.experimental.pallas import tpu as pltpu
from jax.sharding import PartitionSpec as P

MESH = pl.DeviceIdType.MESH
PAD = 16
NZ = 4


def product(window, matrix):
    return lax.dot_general(
        window, matrix, (((1,), (1,)), ((), ())), preferred_element_type=jnp.float32
    )


def on_device_general(newest, earlier, lag_matrices):
    lag_index = lax.axis_index("lag")
    matrix = lag_matrices[0]
    own_steps = newest.shape[0]
    earlier_rows = earlier.shape[0]
    wide_newest, wide_earlier = (
        lax.all_gather(newest, "row", axis=1, tiled=True),
        lax.all_gather(earlier, "row", axis=1, tiled=True),
    )
    history = lax.all_gather(wide_newest, "lag", axis=0, tiled=True)
    record = jnp.concatenate([wide_earlier, history], axis=0)
    window = lax.dynamic_slice_in_dim(
        record, jnp.int32(0) + earlier_rows - lag_index, own_steps * lax.axis_size("lag"), 0
    )
    return lax.psum_scatter(product(window, matrix), "lag", scatter_dimension=0, tiled=True)


def kernel(new_ref, ear_ref, mat_ref, out_ref,
           mat, hist, ebuf, acc, s_d, s_x, s_y, r_d, r_1, r_2,
           loc, zs, zr, xs, xr, ys, yr, ss, sr, es, er, fs, fr):
    lag, row = lax.axis_index("lag"), lax.axis_index("row")
    x, y = lag % 2, lag // 2
    z, core = row // 2, row % 2
    sib = row + 1 - 2 * core
    t0, tx, ty = lag, 2 * y + 1 - x, 2 * (1 - y) + x
    td = 2 * (1 - y) + 1 - x
    steps, width = new_ref.shape
    half = steps // 2
    x_dev, y_dev = {"lag": tx, "row": row}, {"lag": ty, "row": row}
    sib_dev = {"lag": lag, "row": sib}

    mat_copy = pltpu.make_async_copy(mat_ref.at[0], mat, loc.at[0])
    mat_copy.start()

    def rows(t, h, n):
        return pl.ds(pl.multiple_of(PAD + t * steps + h * half, 16), n)

    own_copy = pltpu.make_async_copy(new_ref, hist.at[row, rows(t0, 0, steps)], loc.at[1])
    own_copy.start()
    own_e = pltpu.make_async_copy(ear_ref, ebuf.at[row], loc.at[2])
    own_e.start()

    barrier = pltpu.get_barrier_semaphore()
    for dev in (x_dev, y_dev):
        pl.semaphore_signal(barrier, inc=1, device_id=dev, device_id_type=MESH)
    for j in range(1, 2 * NZ):
        pl.semaphore_signal(barrier, inc=1, device_id={"lag": lag, "row": (row + j) % (2 * NZ)},
                            device_id_type=MESH)
    pl.semaphore_wait(barrier, 2 * NZ + 1)

    def copy(src, dst, ssem, rsem, dev):
        return pltpu.make_async_remote_copy(
            src_ref=src, dst_ref=dst, send_sem=ssem, recv_sem=rsem, device_id=dev,
            device_id_type=MESH)

    def place(r, t, h, n):
        return hist.at[r, rows(t, h, n)]

    z_kind = ((t0, 0, steps), (tx, 0, half), (ty, 1, half))
    x_kind = ((t0, 0, half), (t0, 1, half), (ty, 1, half))
    y_kind = ((t0, 1, half), (t0, 0, half), (tx, 0, half))
    s_kind = tuple((t, 0, steps) for t in (t0, tx, ty, td))
    x_got = ((tx, 0, half), (tx, 1, half), (td, 1, half))
    y_got = ((ty, 1, half), (ty, 0, half), (td, 0, half))

    def fam(zz):
        return 2 * zz + core

    def z_msg(up, zz, m):
        dev = {"lag": lag, "row": row + 2 if up else row - 2}
        ref = place(fam(zz), *z_kind[m])
        return copy(ref, ref, zs.at[int(up), zz, m], zr.at[zz, m], dev)

    def z_own(up):
        dev = {"lag": lag, "row": row + 2 if up else row - 2}
        return copy(new_ref, place(row, *z_kind[0]), zs.at[int(up), z, 0], zr.at[z, 0], dev)

    def x_msg(zz, m):
        ref = place(fam(zz), *x_kind[m])
        return copy(ref, ref, xs.at[zz, m], xr.at[zz, m], x_dev)

    def y_msg(zz, m):
        ref = place(fam(zz), *y_kind[m])
        return copy(ref, ref, ys.at[zz, m], yr.at[zz, m], y_dev)

    def s_msg(zz, m):
        ref = place(fam(zz), *s_kind[m])
        return copy(ref, ref, ss.at[zz, m], sr.at[zz, m], sib_dev)

    def z_wait(zz, m):
        ref = place(fam(zz), *z_kind[m])
        copy(ref, ref, zs.at[0, zz, m], zr.at[zz, m], x_dev).wait_recv()

    def x_wait(zz, m):
        ref = place(fam(zz), *x_got[m])
        copy(ref, ref, xs.at[zz, m], xr.at[zz, m], x_dev).wait_recv()

    def y_wait(zz, m):
        ref = place(fam(zz), *y_got[m])
        copy(ref, ref, ys.at[zz, m], yr.at[zz, m], y_dev).wait_recv()

    def s_wait(zz, m):
        ref = place(2 * zz + 1 - core, *s_kind[m])
        copy(ref, ref, ss.at[zz, m], sr.at[zz, m], sib_dev).wait_recv()

    can_up, can_down = z < NZ - 1, z > 0

    def own_half(h):
        return new_ref.at[pl.ds(h * half, half)]

    @pl.when(can_up)
    def _():
        z_own(True).start()

    @pl.when(can_down)
    def _():
        z_own(False).start()

    own_x = [copy(own_half(h), place(row, t0, h, half), xs.at[z, h], xr.at[z, h], x_dev)
             for h in (0, 1)]
    own_y = [copy(own_half(1 - m), place(row, t0, 1 - m, half), ys.at[z, m], yr.at[z, m], y_dev)
             for m in (0, 1)]
    for m in (0, 1):
        own_x[m].start()
        own_y[m].start()
    copy(new_ref, place(row, t0, 0, steps), ss.at[z, 0], sr.at[z, 0], sib_dev).start()

    def e_msg(j):
        to = (row + j) % (2 * NZ)
        return copy(ear_ref, ebuf.at[row], es.at[j], er.at[row], {"lag": lag, "row": to})

    def e_wait(j):
        frm = (row + j) % (2 * NZ)
        copy(ear_ref, ebuf.at[frm], es.at[j], er.at[frm], sib_dev).wait_recv()

    for j in range(1, 2 * NZ):
        e_msg(j).start()

    wide_up, wide_down = z < NZ - 2, z > 1
    at_end = (z == 0) | (z == NZ - 1)

    def z_on_both(m):
        @pl.when(wide_up)
        def _():
            z_msg(True, z, m).start()

        @pl.when(wide_down)
        def _():
            z_msg(False, z, m).start()

    def arrive(zz, m, up):
        z_wait(zz, m)

        @pl.when(can_up if up else can_down)
        def _():
            z_msg(up, zz, m).start()

        if m == 0:
            x_msg(zz, 1).start()
            y_msg(zz, 1).start()
            s_msg(zz, 0).start()
        elif m == 1:
            y_msg(zz, 2).start()
        else:
            x_msg(zz, 2).start()

    def rest(zz):
        x_wait(zz, 1)
        s_msg(zz, 1).start()
        y_wait(zz, 1)
        s_msg(zz, 2).start()
        x_wait(zz, 2)
        y_wait(zz, 2)
        s_msg(zz, 3).start()

    wide = 512

    def add_plane(zz, n, first=False):
        total = None
        for c in range(2):
            r = 2 * zz + c
            cols = pl.ds(pl.multiple_of(r * width, width), width)
            term = product(hist[r], mat[n, cols])
            total = term if total is None else total + term
        if first:
            acc[:, n] = total
        else:
            acc[:, n] += total

    def whole(zz):
        for m in range(4):
            s_wait(zz, m)

    def some(zz, i, first=False):
        add_plane(zz, pl.ds(i * wide, wide), first)

    x_wait(z, 0)
    z_on_both(1)
    y_msg(z, 2).start()
    y_wait(z, 0)
    z_on_both(2)
    x_msg(z, 2).start()
    inner = jnp.where(z == 0, 1, NZ - 2)

    @pl.when(at_end)
    def _():
        z_wait(inner, 0)
        for m in (0, 1):
            x_msg(inner, m).start()
            y_msg(inner, m).start()
        s_msg(inner, 0).start()

    @pl.when(jnp.logical_not(at_end))
    def _():
        arrive(z - 1, 0, True)
        arrive(z + 1, 0, False)

    own_copy.wait()
    own_e.wait()
    rest(z)
    @pl.when(at_end)
    def _():
        x_wait(inner, 0)
        y_msg(inner, 2).start()
        y_wait(inner, 0)
        x_msg(inner, 2).start()

    @pl.when(jnp.logical_not(at_end))
    def _():
        for m in (1, 2):
            arrive(z - 1, m, True)
            arrive(z + 1, m, False)

    for j in range(1, 2 * NZ):
        e_wait(j)
    chunk = ear_ref.shape[1]
    for r in range(2 * NZ):
        e = ebuf[r].astype(jnp.float32)
        for j in range(width // chunk):
            cut = 4 * j + 4
            piece = e if cut == PAD else jnp.concatenate([e[cut:], e[:cut]], axis=0)
            hist[r, 0:PAD, j * chunk:(j + 1) * chunk] = piece.astype(hist.dtype)
    mat_copy.wait()
    whole(z)
    for i in range(2):
        some(z, i, first=True)
    low = z < NZ // 2
    last = jnp.where(low, NZ - 1, 0)

    def arrive_far(zz, m):
        z_wait(zz, m)
        if m == 0:
            x_msg(zz, 1).start()
            y_msg(zz, 1).start()
            s_msg(zz, 0).start()
        elif m == 1:
            y_msg(zz, 2).start()
        else:
            x_msg(zz, 2).start()

    @pl.when(at_end)
    def _():
        second = jnp.where(low, 2, NZ - 3)
        arrive_far(second, 0)
        rest(inner)
        arrive_far(second, 1)
        arrive_far(second, 2)
        whole(inner)
        for i in range(2):
            some(inner, i)
        arrive_far(last, 0)
        rest(second)
        whole(second)
        for i in range(2):
            some(second, i)
            arrive_far(last, i + 1)

    @pl.when(jnp.logical_not(at_end))
    def _():
        def on(m):
            z_wait(last, m)

            @pl.when(low)
            def _():
                z_msg(False, last, m).start()

            @pl.when(jnp.logical_not(low))
            def _():
                z_msg(True, last, m).start()

            if m == 0:
                x_msg(last, 1).start()
                y_msg(last, 1).start()
                s_msg(last, 0).start()
            elif m == 1:
                y_msg(last, 2).start()
            else:
                x_msg(last, 2).start()

        rest(z - 1)
        rest(z + 1)
        whole(z - 1)
        some(z - 1, 0)
        on(0)
        some(z - 1, 1)
        on(1)
        whole(z + 1)
        some(z + 1, 0)
        on(2)
        some(z + 1, 1)

    rest(last)
    whole(last)

    tile = s_d.shape[2]
    tiles = width // tile

    def shifted(t, h, i):
        start = pl.multiple_of(PAD - 8 + t * steps + h * half, 8)
        part = acc[pl.ds(start, half + 8), i * tile:(i + 1) * tile]
        got = part[8:]
        for k in range(1, 4):
            got = jnp.where(lag == k, part[8 - k:8 - k + half], got)
        return got

    def f_msg(src, dst, h, i, j, dev):
        cut = pl.ds(h * half, half)
        return copy(src.at[i, cut], dst.at[i, cut], fs.at[j, i], fr.at[j, i], dev)

    lo, hi = slice(0, half), slice(half, steps)
    hop_y = [f_msg(s_d, r_d, 0, i, 0, y_dev) for i in range(tiles)]
    hop_x = [f_msg(s_d, r_d, 1, i, 1, x_dev) for i in range(tiles)]
    dir_x = [f_msg(s_x, r_1, 1, i, 2, x_dev) for i in range(tiles)]
    dir_y = [f_msg(s_y, r_1, 0, i, 3, y_dev) for i in range(tiles)]
    last_x = [f_msg(s_x, r_2, 0, i, 4, x_dev) for i in range(tiles)]
    last_y = [f_msg(s_y, r_2, 1, i, 5, y_dev) for i in range(tiles)]
    for i in range(tiles):
        add_plane(last, pl.ds(i * tile, tile))
        s_d[i, lo] = shifted(td, 0, i)
        hop_y[i].start()
        s_d[i, hi] = shifted(td, 1, i)
        hop_x[i].start()
        s_x[i, hi] = shifted(tx, 1, i)
        dir_x[i].start()
        s_y[i, lo] = shifted(ty, 0, i)
        dir_y[i].start()
    for i in range(tiles):
        part_x, part_y = shifted(tx, 0, i), shifted(ty, 1, i)
        hop_y[i].wait_recv()
        s_x[i, lo] = part_x + r_d[i, lo]
        last_x[i].start()
        hop_x[i].wait_recv()
        s_y[i, hi] = part_y + r_d[i, hi]
        last_y[i].start()
    for i in range(tiles):
        n = slice(i * tile, (i + 1) * tile)
        dir_x[i].wait_recv()
        dir_y[i].wait_recv()
        out_ref[lo, n] = shifted(t0, 0, i) + r_1[i, lo]
        out_ref[hi, n] = shifted(t0, 1, i) + r_1[i, hi]
    for i in range(tiles):
        n = slice(i * tile, (i + 1) * tile)
        last_x[i].wait_recv()
        out_ref[lo, n] += r_2[i, lo]
        last_y[i].wait_recv()
        out_ref[hi, n] += r_2[i, hi]

    for group in (hop_y, hop_x, dir_x, dir_y, last_x, last_y):
        for c in group:
            c.wait_send()
    for j in range(1, 2 * NZ):
        e_msg(j).wait_send()
    x_msg(z, 0).wait_send()
    y_msg(z, 0).wait_send()

    @pl.when(at_end)
    def _():
        x_msg(inner, 0).wait_send()
        y_msg(inner, 0).wait_send()

    for zz in range(NZ):
        for m in range(3):
            @pl.when(can_up & (z >= zz) & ((z != zz) | wide_up | (m == 0)))
            def _():
                z_msg(True, zz, m).wait_send()

            @pl.when(can_down & (z <= zz) & ((z != zz) | wide_down | (m == 0)))
            def _():
                z_msg(False, zz, m).wait_send()
        for m in (1, 2):
            x_msg(zz, m).wait_send()
            y_msg(zz, m).wait_send()
        for m in range(4):
            s_msg(zz, m).wait_send()


def on_device(newest, earlier, lag_matrices):
    steps, width = newest.shape
    height = lag_matrices.shape[1]
    count = earlier.shape[0]
    groups = PAD // 4
    packed = jnp.pad(earlier, ((4 - count, 0), (0, 0)))
    packed = packed.reshape(4, groups, width // groups).transpose(1, 0, 2).reshape(PAD, width // groups)
    any_spec = pl.BlockSpec(memory_space=pl.ANY)
    vmem = pl.BlockSpec(memory_space=pltpu.VMEM)
    dma = pltpu.SemaphoreType.DMA
    tile = 256
    block = pltpu.VMEM((height // tile, steps, tile), jnp.float32)
    return pl.pallas_call(
        kernel,
        out_shape=jax.ShapeDtypeStruct((steps, height), jnp.float32),
        in_specs=[any_spec, any_spec, any_spec],
        out_specs=vmem,
        scratch_shapes=[
            pltpu.VMEM((height, 2 * NZ * width), jnp.bfloat16),
            pltpu.VMEM((2 * NZ, PAD + 4 * steps, width), jnp.bfloat16),
            pltpu.VMEM((2 * NZ, PAD, width // groups), jnp.bfloat16),
            pltpu.VMEM((PAD + 4 * steps, height), jnp.float32),
            block, block, block, block, block, block,
            dma((3,)),
            dma((2, NZ, 3)), dma((NZ, 3)),
            dma((NZ, 3)), dma((NZ, 3)),
            dma((NZ, 3)), dma((NZ, 3)),
            dma((NZ, 4)), dma((NZ, 4)),
            dma((2 * NZ,)), dma((2 * NZ,)),
            dma((6, height // tile)), dma((6, height // tile)),
        ],
        compiler_params=pltpu.CompilerParams(
            collective_id=0, has_side_effects=True, vmem_limit_bytes=60 * 1024 * 1024
        ),
        cost_estimate=pl.CostEstimate(
            flops=2 * 4 * steps * height * 2 * NZ * width,
            bytes_accessed=height * 2 * NZ * width * 2, transcendentals=0),
    )(newest, packed, lag_matrices)


def solution(mesh):
    in_specs = (P("lag", "row"), P(None, "row"), P("lag", "row", None))
    out_specs = P("lag", "row")
    fits = mesh.shape["lag"] == 4 and mesh.shape["row"] == 2 * NZ
    return jax.shard_map(
        on_device if fits else on_device_general,
        mesh=mesh, in_specs=in_specs, out_specs=out_specs, check_vma=False
    )
```

```python
import jax
import jax.numpy as jnp
from jax import lax
from jax.experimental import pallas as pl
from jax.experimental.pallas import tpu as pltpu
from jax.sharding import PartitionSpec as P

MESH = pl.DeviceIdType.MESH
PAD = 16
NZ = 4


def product(window, matrix):
    return lax.dot_general(
        window, matrix, (((1,), (1,)), ((), ())), preferred_element_type=jnp.float32
    )


def on_device_general(newest, earlier, lag_matrices):
    lag_index = lax.axis_index("lag")
    matrix = lag_matrices[0]
    own_steps = newest.shape[0]
    earlier_rows = earlier.shape[0]
    wide_newest, wide_earlier = (
        lax.all_gather(newest, "row", axis=1, tiled=True),
        lax.all_gather(earlier, "row", axis=1, tiled=True),
    )
    history = lax.all_gather(wide_newest, "lag", axis=0, tiled=True)
    record = jnp.concatenate([wide_earlier, history], axis=0)
    window = lax.dynamic_slice_in_dim(
        record, jnp.int32(0) + earlier_rows - lag_index, own_steps * lax.axis_size("lag"), 0
    )
    return lax.psum_scatter(product(window, matrix), "lag", scatter_dimension=0, tiled=True)


def kernel(new_ref, ear_ref, mat_ref, out_ref,
           mat, hist, ebuf, acc, s_d, s_x, s_y, r_d, r_1, r_2,
           loc, zs, zr, xs, xr, ys, yr, ss, sr, es, er, fs, fr):
    lag, row = lax.axis_index("lag"), lax.axis_index("row")
    x, y = lag % 2, lag // 2
    z, core = row // 2, row % 2
    sib = row + 1 - 2 * core
    t0, tx, ty = lag, 2 * y + 1 - x, 2 * (1 - y) + x
    td = 2 * (1 - y) + 1 - x
    steps, width = new_ref.shape
    half = steps // 2
    x_dev, y_dev = {"lag": tx, "row": row}, {"lag": ty, "row": row}
    sib_dev = {"lag": lag, "row": sib}

    mat_copy = pltpu.make_async_copy(mat_ref.at[0], mat, loc.at[0])
    mat_copy.start()

    def rows(t, h, n):
        return pl.ds(pl.multiple_of(PAD + t * steps + h * half, 16), n)

    own_copy = pltpu.make_async_copy(new_ref, hist.at[row, rows(t0, 0, steps)], loc.at[1])
    own_copy.start()
    own_e = pltpu.make_async_copy(ear_ref, ebuf.at[row], loc.at[2])
    own_e.start()

    barrier = pltpu.get_barrier_semaphore()
    for dev in (x_dev, y_dev):
        pl.semaphore_signal(barrier, inc=1, device_id=dev, device_id_type=MESH)
    for j in range(1, 2 * NZ):
        pl.semaphore_signal(barrier, inc=1, device_id={"lag": lag, "row": (row + j) % (2 * NZ)},
                            device_id_type=MESH)
    pl.semaphore_wait(barrier, 2 * NZ + 1)

    def copy(src, dst, ssem, rsem, dev):
        return pltpu.make_async_remote_copy(
            src_ref=src, dst_ref=dst, send_sem=ssem, recv_sem=rsem, device_id=dev,
            device_id_type=MESH)

    def place(r, t, h, n):
        return hist.at[r, rows(t, h, n)]

    z_kind = ((t0, 0, steps), (tx, 0, half), (ty, 1, half))
    x_kind = ((t0, 0, half), (t0, 1, half), (ty, 1, half))
    y_kind = ((t0, 1, half), (t0, 0, half), (tx, 0, half))
    s_kind = tuple((t, 0, steps) for t in (t0, tx, ty, td))
    x_got = ((tx, 0, half), (tx, 1, half), (td, 1, half))
    y_got = ((ty, 1, half), (ty, 0, half), (td, 0, half))

    def fam(zz):
        return 2 * zz + core

    def z_msg(up, zz, m):
        dev = {"lag": lag, "row": row + 2 if up else row - 2}
        ref = place(fam(zz), *z_kind[m])
        return copy(ref, ref, zs.at[int(up), zz, m], zr.at[zz, m], dev)

    def z_own(up):
        dev = {"lag": lag, "row": row + 2 if up else row - 2}
        return copy(new_ref, place(row, *z_kind[0]), zs.at[int(up), z, 0], zr.at[z, 0], dev)

    def x_msg(zz, m):
        ref = place(fam(zz), *x_kind[m])
        return copy(ref, ref, xs.at[zz, m], xr.at[zz, m], x_dev)

    def y_msg(zz, m):
        ref = place(fam(zz), *y_kind[m])
        return copy(ref, ref, ys.at[zz, m], yr.at[zz, m], y_dev)

    def s_msg(zz, m):
        ref = place(fam(zz), *s_kind[m])
        return copy(ref, ref, ss.at[zz, m], sr.at[zz, m], sib_dev)

    def z_wait(zz, m):
        ref = place(fam(zz), *z_kind[m])
        copy(ref, ref, zs.at[0, zz, m], zr.at[zz, m], x_dev).wait_recv()

    def x_wait(zz, m):
        ref = place(fam(zz), *x_got[m])
        copy(ref, ref, xs.at[zz, m], xr.at[zz, m], x_dev).wait_recv()

    def y_wait(zz, m):
        ref = place(fam(zz), *y_got[m])
        copy(ref, ref, ys.at[zz, m], yr.at[zz, m], y_dev).wait_recv()

    def s_wait(zz, m):
        ref = place(2 * zz + 1 - core, *s_kind[m])
        copy(ref, ref, ss.at[zz, m], sr.at[zz, m], sib_dev).wait_recv()

    can_up, can_down = z < NZ - 1, z > 0

    def own_half(h):
        return new_ref.at[pl.ds(h * half, half)]

    @pl.when(can_up)
    def _():
        z_own(True).start()

    @pl.when(can_down)
    def _():
        z_own(False).start()

    own_x = [copy(own_half(h), place(row, t0, h, half), xs.at[z, h], xr.at[z, h], x_dev)
             for h in (0, 1)]
    own_y = [copy(own_half(1 - m), place(row, t0, 1 - m, half), ys.at[z, m], yr.at[z, m], y_dev)
             for m in (0, 1)]
    for m in (0, 1):
        own_x[m].start()
        own_y[m].start()
    copy(new_ref, place(row, t0, 0, steps), ss.at[z, 0], sr.at[z, 0], sib_dev).start()

    def e_msg(j):
        to = (row + j) % (2 * NZ)
        return copy(ear_ref, ebuf.at[row], es.at[j], er.at[row], {"lag": lag, "row": to})

    def e_wait(j):
        frm = (row + j) % (2 * NZ)
        copy(ear_ref, ebuf.at[frm], es.at[j], er.at[frm], sib_dev).wait_recv()

    for j in range(1, 2 * NZ):
        e_msg(j).start()

    wide_up, wide_down = z < NZ - 2, z > 1
    at_end = (z == 0) | (z == NZ - 1)

    def z_on_both(m):
        @pl.when(wide_up)
        def _():
            z_msg(True, z, m).start()

        @pl.when(wide_down)
        def _():
            z_msg(False, z, m).start()

    def arrive(zz, m, up):
        z_wait(zz, m)

        @pl.when(can_up if up else can_down)
        def _():
            z_msg(up, zz, m).start()

        if m == 0:
            x_msg(zz, 1).start()
            y_msg(zz, 1).start()
            s_msg(zz, 0).start()
        elif m == 1:
            y_msg(zz, 2).start()
        else:
            x_msg(zz, 2).start()

    def rest(zz):
        x_wait(zz, 1)
        s_msg(zz, 1).start()
        y_wait(zz, 1)
        s_msg(zz, 2).start()
        x_wait(zz, 2)
        y_wait(zz, 2)
        s_msg(zz, 3).start()

    wide = 512

    def add_plane(zz, n, first=False):
        total = None
        for c in range(2):
            r = 2 * zz + c
            cols = pl.ds(pl.multiple_of(r * width, width), width)
            term = product(hist[r], mat[n, cols])
            total = term if total is None else total + term
        if first:
            acc[:, n] = total
        else:
            acc[:, n] += total

    def whole(zz):
        for m in range(4):
            s_wait(zz, m)

    def some(zz, i, first=False):
        add_plane(zz, pl.ds(i * wide, wide), first)

    x_wait(z, 0)
    z_on_both(1)
    y_msg(z, 2).start()
    y_wait(z, 0)
    z_on_both(2)
    x_msg(z, 2).start()
    inner = jnp.where(z == 0, 1, NZ - 2)

    @pl.when(at_end)
    def _():
        z_wait(inner, 0)
        for m in (0, 1):
            x_msg(inner, m).start()
            y_msg(inner, m).start()
        s_msg(inner, 0).start()

    @pl.when(jnp.logical_not(at_end))
    def _():
        arrive(z - 1, 0, True)
        arrive(z + 1, 0, False)

    own_copy.wait()
    own_e.wait()
    rest(z)
    @pl.when(at_end)
    def _():
        x_wait(inner, 0)
        y_msg(inner, 2).start()
        y_wait(inner, 0)
        x_msg(inner, 2).start()

    @pl.when(jnp.logical_not(at_end))
    def _():
        for m in (1, 2):
            arrive(z - 1, m, True)
            arrive(z + 1, m, False)

    for j in range(1, 2 * NZ):
        e_wait(j)
    chunk = ear_ref.shape[1]
    for r in range(2 * NZ):
        e = ebuf[r].astype(jnp.float32)
        for j in range(width // chunk):
            cut = 4 * j + 4
            piece = e if cut == PAD else jnp.concatenate([e[cut:], e[:cut]], axis=0)
            hist[r, 0:PAD, j * chunk:(j + 1) * chunk] = piece.astype(hist.dtype)
    mat_copy.wait()
    whole(z)
    for i in range(2):
        some(z, i, first=True)
    low = z < NZ // 2
    last = jnp.where(low, NZ - 1, 0)

    def arrive_far(zz, m):
        z_wait(zz, m)
        if m == 0:
            x_msg(zz, 1).start()
            y_msg(zz, 1).start()
            s_msg(zz, 0).start()
        elif m == 1:
            y_msg(zz, 2).start()
        else:
            x_msg(zz, 2).start()

    @pl.when(at_end)
    def _():
        second = jnp.where(low, 2, NZ - 3)
        arrive_far(second, 0)
        rest(inner)
        arrive_far(second, 1)
        arrive_far(second, 2)
        whole(inner)
        for i in range(2):
            some(inner, i)
        arrive_far(last, 0)
        rest(second)
        whole(second)
        arrive_far(last, 1)
        arrive_far(last, 2)
        for i in range(2):
            some(second, i)

    @pl.when(jnp.logical_not(at_end))
    def _():
        def on(m):
            z_wait(last, m)

            @pl.when(low)
            def _():
                z_msg(False, last, m).start()

            @pl.when(jnp.logical_not(low))
            def _():
                z_msg(True, last, m).start()

            if m == 0:
                x_msg(last, 1).start()
                y_msg(last, 1).start()
                s_msg(last, 0).start()
            elif m == 1:
                y_msg(last, 2).start()
            else:
                x_msg(last, 2).start()

        on(0)
        rest(z - 1)
        rest(z + 1)
        on(1)
        whole(z - 1)
        some(z - 1, 0)
        on(2)
        some(z - 1, 1)
        whole(z + 1)
        for i in range(2):
            some(z + 1, i)

    rest(last)
    whole(last)

    tile = s_d.shape[2]
    tiles = width // tile

    def shifted(t, h, i):
        start = pl.multiple_of(PAD - 8 + t * steps + h * half, 8)
        part = acc[pl.ds(start, half + 8), i * tile:(i + 1) * tile]
        got = part[8:]
        for k in range(1, 4):
            got = jnp.where(lag == k, part[8 - k:8 - k + half], got)
        return got

    def f_msg(src, dst, h, i, j, dev):
        cut = pl.ds(h * half, half)
        return copy(src.at[i, cut], dst.at[i, cut], fs.at[j, i], fr.at[j, i], dev)

    lo, hi = slice(0, half), slice(half, steps)
    hop_y = [f_msg(s_d, r_d, 0, i, 0, y_dev) for i in range(tiles)]
    hop_x = [f_msg(s_d, r_d, 1, i, 1, x_dev) for i in range(tiles)]
    dir_x = [f_msg(s_x, r_1, 1, i, 2, x_dev) for i in range(tiles)]
    dir_y = [f_msg(s_y, r_1, 0, i, 3, y_dev) for i in range(tiles)]
    last_x = [f_msg(s_x, r_2, 0, i, 4, x_dev) for i in range(tiles)]
    last_y = [f_msg(s_y, r_2, 1, i, 5, y_dev) for i in range(tiles)]
    for i in range(tiles):
        add_plane(last, pl.ds(i * tile, tile))
        s_d[i, lo] = shifted(td, 0, i)
        hop_y[i].start()
        s_d[i, hi] = shifted(td, 1, i)
        hop_x[i].start()
        s_x[i, hi] = shifted(tx, 1, i)
        dir_x[i].start()
        s_y[i, lo] = shifted(ty, 0, i)
        dir_y[i].start()
    for i in range(tiles):
        part_x, part_y = shifted(tx, 0, i), shifted(ty, 1, i)
        hop_y[i].wait_recv()
        s_x[i, lo] = part_x + r_d[i, lo]
        last_x[i].start()
        hop_x[i].wait_recv()
        s_y[i, hi] = part_y + r_d[i, hi]
        last_y[i].start()
    for i in range(tiles):
        n = slice(i * tile, (i + 1) * tile)
        dir_x[i].wait_recv()
        dir_y[i].wait_recv()
        out_ref[lo, n] = shifted(t0, 0, i) + r_1[i, lo]
        out_ref[hi, n] = shifted(t0, 1, i) + r_1[i, hi]
    for i in range(tiles):
        n = slice(i * tile, (i + 1) * tile)
        last_x[i].wait_recv()
        out_ref[lo, n] += r_2[i, lo]
        last_y[i].wait_recv()
        out_ref[hi, n] += r_2[i, hi]

    for group in (hop_y, hop_x, dir_x, dir_y, last_x, last_y):
        for c in group:
            c.wait_send()
    for j in range(1, 2 * NZ):
        e_msg(j).wait_send()
    x_msg(z, 0).wait_send()
    y_msg(z, 0).wait_send()

    @pl.when(at_end)
    def _():
        x_msg(inner, 0).wait_send()
        y_msg(inner, 0).wait_send()

    for zz in range(NZ):
        for m in range(3):
            @pl.when(can_up & (z >= zz) & ((z != zz) | wide_up | (m == 0)))
            def _():
                z_msg(True, zz, m).wait_send()

            @pl.when(can_down & (z <= zz) & ((z != zz) | wide_down | (m == 0)))
            def _():
                z_msg(False, zz, m).wait_send()
        for m in (1, 2):
            x_msg(zz, m).wait_send()
            y_msg(zz, m).wait_send()
        for m in range(4):
            s_msg(zz, m).wait_send()


def on_device(newest, earlier, lag_matrices):
    steps, width = newest.shape
    height = lag_matrices.shape[1]
    count = earlier.shape[0]
    groups = PAD // 4
    packed = jnp.pad(earlier, ((4 - count, 0), (0, 0)))
    packed = packed.reshape(4, groups, width // groups).transpose(1, 0, 2).reshape(PAD, width // groups)
    any_spec = pl.BlockSpec(memory_space=pl.ANY)
    vmem = pl.BlockSpec(memory_space=pltpu.VMEM)
    dma = pltpu.SemaphoreType.DMA
    tile = 256
    block = pltpu.VMEM((height // tile, steps, tile), jnp.float32)
    return pl.pallas_call(
        kernel,
        out_shape=jax.ShapeDtypeStruct((steps, height), jnp.float32),
        in_specs=[any_spec, any_spec, any_spec],
        out_specs=vmem,
        scratch_shapes=[
            pltpu.VMEM((height, 2 * NZ * width), jnp.bfloat16),
            pltpu.VMEM((2 * NZ, PAD + 4 * steps, width), jnp.bfloat16),
            pltpu.VMEM((2 * NZ, PAD, width // groups), jnp.bfloat16),
            pltpu.VMEM((PAD + 4 * steps, height), jnp.float32),
            block, block, block, block, block, block,
            dma((3,)),
            dma((2, NZ, 3)), dma((NZ, 3)),
            dma((NZ, 3)), dma((NZ, 3)),
            dma((NZ, 3)), dma((NZ, 3)),
            dma((NZ, 4)), dma((NZ, 4)),
            dma((2 * NZ,)), dma((2 * NZ,)),
            dma((6, height // tile)), dma((6, height // tile)),
        ],
        compiler_params=pltpu.CompilerParams(
            collective_id=0, has_side_effects=True, vmem_limit_bytes=48 * 1024 * 1024
        ),
        cost_estimate=pl.CostEstimate(
            flops=2 * 4 * steps * height * 2 * NZ * width,
            bytes_accessed=height * 2 * NZ * width * 2, transcendentals=0),
    )(newest, packed, lag_matrices)


def solution(mesh):
    in_specs = (P("lag", "row"), P(None, "row"), P("lag", "row", None))
    out_specs = P("lag", "row")
    fits = mesh.shape["lag"] == 4 and mesh.shape["row"] == 2 * NZ
    return jax.shard_map(
        on_device if fits else on_device_general,
        mesh=mesh, in_specs=in_specs, out_specs=out_specs, check_vma=False
    )
```

```python
import jax
import jax.numpy as jnp
from jax import lax
from jax.experimental import pallas as pl
from jax.experimental.pallas import tpu as pltpu
from jax.sharding import PartitionSpec as P

MESH = pl.DeviceIdType.MESH
PAD = 16
NZ = 4


def product(window, matrix):
    return lax.dot_general(
        window, matrix, (((1,), (1,)), ((), ())), preferred_element_type=jnp.float32
    )


def on_device_general(newest, earlier, lag_matrices):
    lag_index = lax.axis_index("lag")
    matrix = lag_matrices[0]
    own_steps = newest.shape[0]
    earlier_rows = earlier.shape[0]
    wide_newest, wide_earlier = (
        lax.all_gather(newest, "row", axis=1, tiled=True),
        lax.all_gather(earlier, "row", axis=1, tiled=True),
    )
    history = lax.all_gather(wide_newest, "lag", axis=0, tiled=True)
    record = jnp.concatenate([wide_earlier, history], axis=0)
    window = lax.dynamic_slice_in_dim(
        record, jnp.int32(0) + earlier_rows - lag_index, own_steps * lax.axis_size("lag"), 0
    )
    return lax.psum_scatter(product(window, matrix), "lag", scatter_dimension=0, tiled=True)


def kernel(new_ref, ear_ref, mat_ref, out_ref,
           mat, hist, ebuf, acc, s_d, s_x, s_y, r_d, r_1, r_2,
           loc, zs, zr, xs, xr, ys, yr, ss, sr, es, er, fs, fr):
    lag, row = lax.axis_index("lag"), lax.axis_index("row")
    x, y = lag % 2, lag // 2
    z, core = row // 2, row % 2
    sib = row + 1 - 2 * core
    t0, tx, ty = lag, 2 * y + 1 - x, 2 * (1 - y) + x
    td = 2 * (1 - y) + 1 - x
    steps, width = new_ref.shape
    half = steps // 2
    quarter = steps // 4
    x_dev, y_dev = {"lag": tx, "row": row}, {"lag": ty, "row": row}
    sib_dev = {"lag": lag, "row": sib}

    mat_copy = pltpu.make_async_copy(mat_ref.at[0], mat, loc.at[0])
    mat_copy.start()

    def rows(t, q, n):
        return pl.ds(pl.multiple_of(PAD + t * steps + q * quarter, 16), n * quarter)

    own_copy = pltpu.make_async_copy(new_ref, hist.at[row, rows(t0, 0, 4)], loc.at[1])
    own_copy.start()
    own_e = pltpu.make_async_copy(ear_ref, ebuf.at[row], loc.at[2])
    own_e.start()

    barrier = pltpu.get_barrier_semaphore()
    for dev in (x_dev, y_dev):
        pl.semaphore_signal(barrier, inc=1, device_id=dev, device_id_type=MESH)
    for j in range(1, 2 * NZ):
        pl.semaphore_signal(barrier, inc=1, device_id={"lag": lag, "row": (row + j) % (2 * NZ)},
                            device_id_type=MESH)
    pl.semaphore_wait(barrier, 2 * NZ + 1)

    def copy(src, dst, ssem, rsem, dev):
        return pltpu.make_async_remote_copy(
            src_ref=src, dst_ref=dst, send_sem=ssem, recv_sem=rsem, device_id=dev,
            device_id_type=MESH)

    def place(r, t, q, n):
        return hist.at[r, rows(t, q, n)]

    z_kind = ((t0, 0, 2), (t0, 2, 2), (tx, 0, 1), (ty, 2, 1), (tx, 1, 1), (ty, 3, 1))
    x_kind = ((t0, 0, 2), (t0, 2, 2), (ty, 2, 1), (ty, 3, 1))
    y_kind = ((t0, 2, 2), (t0, 0, 2), (tx, 0, 1), (tx, 1, 1))
    s_kind = tuple((t, 0, 4) for t in (t0, tx, ty, td))
    x_got = ((tx, 0, 2), (tx, 2, 2), (td, 2, 1), (td, 3, 1))
    y_got = ((ty, 2, 2), (ty, 0, 2), (td, 0, 1), (td, 1, 1))

    def fam(zz):
        return 2 * zz + core

    def z_msg(up, zz, m):
        dev = {"lag": lag, "row": row + 2 if up else row - 2}
        ref = place(fam(zz), *z_kind[m])
        return copy(ref, ref, zs.at[int(up), zz, m], zr.at[zz, m], dev)

    def z_own(up, h):
        dev = {"lag": lag, "row": row + 2 if up else row - 2}
        return copy(own_half(h), place(row, *z_kind[h]), zs.at[int(up), z, h], zr.at[z, h], dev)

    def x_msg(zz, m):
        ref = place(fam(zz), *x_kind[m])
        return copy(ref, ref, xs.at[zz, m], xr.at[zz, m], x_dev)

    def y_msg(zz, m):
        ref = place(fam(zz), *y_kind[m])
        return copy(ref, ref, ys.at[zz, m], yr.at[zz, m], y_dev)

    def s_msg(zz, m):
        ref = place(fam(zz), *s_kind[m])
        return copy(ref, ref, ss.at[zz, m], sr.at[zz, m], sib_dev)

    def z_wait(zz, m):
        ref = place(fam(zz), *z_kind[m])
        copy(ref, ref, zs.at[0, zz, m], zr.at[zz, m], x_dev).wait_recv()

    def x_wait(zz, m):
        ref = place(fam(zz), *x_got[m])
        copy(ref, ref, xs.at[zz, m], xr.at[zz, m], x_dev).wait_recv()

    def y_wait(zz, m):
        ref = place(fam(zz), *y_got[m])
        copy(ref, ref, ys.at[zz, m], yr.at[zz, m], y_dev).wait_recv()

    def s_wait(zz, m):
        ref = place(2 * zz + 1 - core, *s_kind[m])
        copy(ref, ref, ss.at[zz, m], sr.at[zz, m], sib_dev).wait_recv()

    can_up, can_down = z < NZ - 1, z > 0

    def own_half(h):
        return new_ref.at[pl.ds(h * half, half)]

    for h in (0, 1):
        @pl.when(can_up)
        def _():
            z_own(True, h).start()

        @pl.when(can_down)
        def _():
            z_own(False, h).start()

    own_x = [copy(own_half(h), place(row, t0, 2 * h, 2), xs.at[z, h], xr.at[z, h], x_dev)
             for h in (0, 1)]
    own_y = [copy(own_half(1 - m), place(row, t0, 2 - 2 * m, 2), ys.at[z, m], yr.at[z, m], y_dev)
             for m in (0, 1)]
    for m in (0, 1):
        own_x[m].start()
        own_y[m].start()
    copy(new_ref, place(row, t0, 0, 4), ss.at[z, 0], sr.at[z, 0], sib_dev).start()

    def e_msg(j):
        to = (row + j) % (2 * NZ)
        return copy(ear_ref, ebuf.at[row], es.at[j], er.at[row], {"lag": lag, "row": to})

    def e_wait(j):
        frm = (row + j) % (2 * NZ)
        copy(ear_ref, ebuf.at[frm], es.at[j], er.at[frm], sib_dev).wait_recv()

    for j in range(1, 2 * NZ):
        e_msg(j).start()

    wide_up, wide_down = z < NZ - 2, z > 1
    at_end = (z == 0) | (z == NZ - 1)

    def z_on_both(m):
        @pl.when(wide_up)
        def _():
            z_msg(True, z, m).start()

        @pl.when(wide_down)
        def _():
            z_msg(False, z, m).start()

    def share(zz, m):
        if m % 2 == 0:
            y_msg(zz, 1 + m // 2).start()
        else:
            x_msg(zz, 1 + m // 2).start()
        if m == 1:
            s_msg(zz, 0).start()

    def arrive(zz, m, up):
        z_wait(zz, m)

        @pl.when(can_up if up else can_down)
        def _():
            z_msg(up, zz, m).start()

        share(zz, m)

    def rest(zz):
        x_wait(zz, 1)
        s_msg(zz, 1).start()
        y_wait(zz, 1)
        s_msg(zz, 2).start()
        for m in (2, 3):
            x_wait(zz, m)
            y_wait(zz, m)
        s_msg(zz, 3).start()

    wide = 512

    def add_plane(zz, n, first=False):
        total = None
        for c in range(2):
            r = 2 * zz + c
            cols = pl.ds(pl.multiple_of(r * width, width), width)
            term = product(hist[r], mat[n, cols])
            total = term if total is None else total + term
        if first:
            acc[:, n] = total
        else:
            acc[:, n] += total

    def whole(zz):
        for m in range(4):
            s_wait(zz, m)

    def some(zz, i, first=False):
        add_plane(zz, pl.ds(i * wide, wide), first)

    inner = jnp.where(z == 0, 1, NZ - 2)
    between = jnp.logical_not(at_end)

    def beside(m):
        @pl.when(at_end)
        def _():
            z_wait(inner, m)
            x_msg(inner, m).start()
            y_msg(inner, 1 - m).start()
            if m == 1:
                s_msg(inner, 0).start()

        @pl.when(between)
        def _():
            arrive(z - 1, m, True)
            arrive(z + 1, m, False)

    beside(0)
    x_wait(z, 0)
    z_on_both(2)
    y_msg(z, 2).start()
    y_wait(z, 0)
    z_on_both(3)
    x_msg(z, 2).start()
    z_on_both(4)
    y_msg(z, 3).start()
    z_on_both(5)
    x_msg(z, 3).start()
    beside(1)
    own_copy.wait()
    own_e.wait()
    rest(z)
    @pl.when(at_end)
    def _():
        x_wait(inner, 0)
        y_msg(inner, 2).start()
        y_wait(inner, 0)
        x_msg(inner, 2).start()
        y_msg(inner, 3).start()
        x_msg(inner, 3).start()

    @pl.when(between)
    def _():
        for m in range(2, 6):
            arrive(z - 1, m, True)
            arrive(z + 1, m, False)

    for j in range(1, 2 * NZ):
        e_wait(j)
    chunk = ear_ref.shape[1]
    for r in range(2 * NZ):
        e = ebuf[r].astype(jnp.float32)
        for j in range(width // chunk):
            cut = 4 * j + 4
            piece = e if cut == PAD else jnp.concatenate([e[cut:], e[:cut]], axis=0)
            hist[r, 0:PAD, j * chunk:(j + 1) * chunk] = piece.astype(hist.dtype)
    mat_copy.wait()
    whole(z)
    for i in range(2):
        some(z, i, first=True)
    low = z < NZ // 2
    last = jnp.where(low, NZ - 1, 0)

    @pl.when(at_end)
    def _():
        second = jnp.where(low, 2, NZ - 3)

        def far(zz, *ms):
            for m in ms:
                z_wait(zz, m)
                share(zz, m)

        far(second, 0, 1, 2, 3)
        rest(inner)
        far(second, 4, 5)
        whole(inner)
        for i in range(2):
            some(inner, i)
        far(last, 0, 1)
        rest(second)
        far(last, 2, 3)
        whole(second)
        some(second, 0)
        far(last, 4, 5)
        some(second, 1)

    @pl.when(between)
    def _():
        def on(*ms):
            for m in ms:
                z_wait(last, m)

                @pl.when(low)
                def _():
                    z_msg(False, last, m).start()

                @pl.when(jnp.logical_not(low))
                def _():
                    z_msg(True, last, m).start()

                share(last, m)

        on(0, 1, 2, 3)
        rest(z - 1)
        rest(z + 1)
        on(4, 5)
        for zz in (z - 1, z + 1):
            whole(zz)
            for i in range(2):
                some(zz, i)

    rest(last)
    whole(last)

    tile = s_d.shape[2]
    tiles = width // tile

    def shifted(t, h, i):
        start = pl.multiple_of(PAD - 8 + t * steps + h * half, 8)
        part = acc[pl.ds(start, half + 8), i * tile:(i + 1) * tile]
        got = part[8:]
        for k in range(1, 4):
            got = jnp.where(lag == k, part[8 - k:8 - k + half], got)
        return got

    def f_msg(src, dst, h, i, j, dev):
        cut = pl.ds(h * half, half)
        return copy(src.at[i, cut], dst.at[i, cut], fs.at[j, i], fr.at[j, i], dev)

    lo, hi = slice(0, half), slice(half, steps)
    hop_y = [f_msg(s_d, r_d, 0, i, 0, y_dev) for i in range(tiles)]
    hop_x = [f_msg(s_d, r_d, 1, i, 1, x_dev) for i in range(tiles)]
    dir_x = [f_msg(s_x, r_1, 1, i, 2, x_dev) for i in range(tiles)]
    dir_y = [f_msg(s_y, r_1, 0, i, 3, y_dev) for i in range(tiles)]
    last_x = [f_msg(s_x, r_2, 0, i, 4, x_dev) for i in range(tiles)]
    last_y = [f_msg(s_y, r_2, 1, i, 5, y_dev) for i in range(tiles)]
    for i in range(tiles):
        add_plane(last, pl.ds(i * tile, tile))
        s_d[i, lo] = shifted(td, 0, i)
        hop_y[i].start()
        s_d[i, hi] = shifted(td, 1, i)
        hop_x[i].start()
        s_x[i, hi] = shifted(tx, 1, i)
        dir_x[i].start()
        s_y[i, lo] = shifted(ty, 0, i)
        dir_y[i].start()
    for i in range(tiles):
        part_x, part_y = shifted(tx, 0, i), shifted(ty, 1, i)
        hop_y[i].wait_recv()
        s_x[i, lo] = part_x + r_d[i, lo]
        last_x[i].start()
        hop_x[i].wait_recv()
        s_y[i, hi] = part_y + r_d[i, hi]
        last_y[i].start()
    for i in range(tiles):
        n = slice(i * tile, (i + 1) * tile)
        dir_x[i].wait_recv()
        dir_y[i].wait_recv()
        out_ref[lo, n] = shifted(t0, 0, i) + r_1[i, lo]
        out_ref[hi, n] = shifted(t0, 1, i) + r_1[i, hi]
    for i in range(tiles):
        n = slice(i * tile, (i + 1) * tile)
        last_x[i].wait_recv()
        out_ref[lo, n] += r_2[i, lo]
        last_y[i].wait_recv()
        out_ref[hi, n] += r_2[i, hi]

    for group in (hop_y, hop_x, dir_x, dir_y, last_x, last_y):
        for c in group:
            c.wait_send()
    for j in range(1, 2 * NZ):
        e_msg(j).wait_send()
    x_msg(z, 0).wait_send()
    y_msg(z, 0).wait_send()

    @pl.when(at_end)
    def _():
        x_msg(inner, 0).wait_send()
        y_msg(inner, 0).wait_send()

    for zz in range(NZ):
        for m in range(6):
            @pl.when(can_up & (z >= zz) & ((z != zz) | wide_up | (m < 2)))
            def _():
                z_msg(True, zz, m).wait_send()

            @pl.when(can_down & (z <= zz) & ((z != zz) | wide_down | (m < 2)))
            def _():
                z_msg(False, zz, m).wait_send()
        for m in (1, 2, 3):
            x_msg(zz, m).wait_send()
            y_msg(zz, m).wait_send()
        for m in range(4):
            s_msg(zz, m).wait_send()


def on_device(newest, earlier, lag_matrices):
    steps, width = newest.shape
    height = lag_matrices.shape[1]
    count = earlier.shape[0]
    groups = PAD // 4
    packed = jnp.pad(earlier, ((4 - count, 0), (0, 0)))
    packed = packed.reshape(4, groups, width // groups).transpose(1, 0, 2).reshape(PAD, width // groups)
    any_spec = pl.BlockSpec(memory_space=pl.ANY)
    vmem = pl.BlockSpec(memory_space=pltpu.VMEM)
    dma = pltpu.SemaphoreType.DMA
    tile = 256
    block = pltpu.VMEM((height // tile, steps, tile), jnp.float32)
    return pl.pallas_call(
        kernel,
        out_shape=jax.ShapeDtypeStruct((steps, height), jnp.float32),
        in_specs=[pl.BlockSpec(memory_space=pltpu.HBM), any_spec, any_spec],
        out_specs=vmem,
        scratch_shapes=[
            pltpu.VMEM((height, 2 * NZ * width), jnp.bfloat16),
            pltpu.VMEM((2 * NZ, PAD + 4 * steps, width), jnp.bfloat16),
            pltpu.VMEM((2 * NZ, PAD, width // groups), jnp.bfloat16),
            pltpu.VMEM((PAD + 4 * steps, height), jnp.float32),
            block, block, block, block, block, block,
            dma((3,)),
            dma((2, NZ, 6)), dma((NZ, 6)),
            dma((NZ, 4)), dma((NZ, 4)),
            dma((NZ, 4)), dma((NZ, 4)),
            dma((NZ, 4)), dma((NZ, 4)),
            dma((2 * NZ,)), dma((2 * NZ,)),
            dma((6, height // tile)), dma((6, height // tile)),
        ],
        compiler_params=pltpu.CompilerParams(
            collective_id=0, has_side_effects=True, vmem_limit_bytes=48 * 1024 * 1024
        ),
        cost_estimate=pl.CostEstimate(
            flops=2 * 4 * steps * height * 2 * NZ * width,
            bytes_accessed=height * 2 * NZ * width * 2, transcendentals=0),
    )(newest, packed, lag_matrices)


def solution(mesh):
    in_specs = (P("lag", "row"), P(None, "row"), P("lag", "row", None))
    out_specs = P("lag", "row")
    fits = mesh.shape["lag"] == 4 and mesh.shape["row"] == 2 * NZ
    return jax.shard_map(
        on_device if fits else on_device_general,
        mesh=mesh, in_specs=in_specs, out_specs=out_specs, check_vma=False
    )
```

```python
import jax
import jax.numpy as jnp
from jax import lax
from jax.experimental import pallas as pl
from jax.experimental.pallas import tpu as pltpu
from jax.sharding import PartitionSpec as P

MESH = pl.DeviceIdType.MESH
PAD = 16
NZ = 4


def product(window, matrix):
    return lax.dot_general(
        window, matrix, (((1,), (1,)), ((), ())), preferred_element_type=jnp.float32
    )


def on_device_general(newest, earlier, lag_matrices):
    lag_index = lax.axis_index("lag")
    matrix = lag_matrices[0]
    own_steps = newest.shape[0]
    earlier_rows = earlier.shape[0]
    wide_newest, wide_earlier = (
        lax.all_gather(newest, "row", axis=1, tiled=True),
        lax.all_gather(earlier, "row", axis=1, tiled=True),
    )
    history = lax.all_gather(wide_newest, "lag", axis=0, tiled=True)
    record = jnp.concatenate([wide_earlier, history], axis=0)
    window = lax.dynamic_slice_in_dim(
        record, jnp.int32(0) + earlier_rows - lag_index, own_steps * lax.axis_size("lag"), 0
    )
    return lax.psum_scatter(product(window, matrix), "lag", scatter_dimension=0, tiled=True)


def kernel(new_ref, ear_ref, mat_ref, out_ref,
           mat, hist, ebuf, acc, s_d, s_x, s_y, r_d, r_1, r_2,
           loc, zs, zr, xs, xr, ys, yr, ss, sr, es, er, fs, fr):
    lag, row = lax.axis_index("lag"), lax.axis_index("row")
    x, y = lag % 2, lag // 2
    z, core = row // 2, row % 2
    sib = row + 1 - 2 * core
    t0, tx, ty = lag, 2 * y + 1 - x, 2 * (1 - y) + x
    td = 2 * (1 - y) + 1 - x
    steps, width = new_ref.shape
    half = steps // 2
    x_dev, y_dev = {"lag": tx, "row": row}, {"lag": ty, "row": row}
    sib_dev = {"lag": lag, "row": sib}

    mat_copy = pltpu.make_async_copy(mat_ref.at[0], mat, loc.at[0])
    mat_copy.start()

    def rows(t, h, n):
        return pl.ds(pl.multiple_of(PAD + t * steps + h * half, 16), n)

    own_copy = pltpu.make_async_copy(new_ref, hist.at[row, rows(t0, 0, steps)], loc.at[1])
    own_copy.start()
    own_e = pltpu.make_async_copy(ear_ref, ebuf.at[row], loc.at[2])
    own_e.start()

    barrier = pltpu.get_barrier_semaphore()
    for dev in (x_dev, y_dev):
        pl.semaphore_signal(barrier, inc=1, device_id=dev, device_id_type=MESH)
    for j in range(1, 2 * NZ):
        pl.semaphore_signal(barrier, inc=1, device_id={"lag": lag, "row": (row + j) % (2 * NZ)},
                            device_id_type=MESH)
    pl.semaphore_wait(barrier, 2 * NZ + 1)

    def copy(src, dst, ssem, rsem, dev):
        return pltpu.make_async_remote_copy(
            src_ref=src, dst_ref=dst, send_sem=ssem, recv_sem=rsem, device_id=dev,
            device_id_type=MESH)

    def place(r, t, h, n):
        return hist.at[r, rows(t, h, n)]

    z_kind = ((t0, 0, steps), (tx, 0, half), (ty, 1, half))
    x_kind = ((t0, 0, half), (t0, 1, half), (ty, 1, half))
    y_kind = ((t0, 1, half), (t0, 0, half), (tx, 0, half))
    s_kind = tuple((t, 0, steps) for t in (t0, tx, ty, td))
    x_got = ((tx, 0, half), (tx, 1, half), (td, 1, half))
    y_got = ((ty, 1, half), (ty, 0, half), (td, 0, half))

    def fam(zz):
        return 2 * zz + core

    def z_msg(up, zz, m):
        dev = {"lag": lag, "row": row + 2 if up else row - 2}
        ref = place(fam(zz), *z_kind[m])
        return copy(ref, ref, zs.at[int(up), zz, m], zr.at[zz, m], dev)

    def z_own(up):
        dev = {"lag": lag, "row": row + 2 if up else row - 2}
        return copy(new_ref, place(row, *z_kind[0]), zs.at[int(up), z, 0], zr.at[z, 0], dev)

    def x_msg(zz, m):
        ref = place(fam(zz), *x_kind[m])
        return copy(ref, ref, xs.at[zz, m], xr.at[zz, m], x_dev)

    def y_msg(zz, m):
        ref = place(fam(zz), *y_kind[m])
        return copy(ref, ref, ys.at[zz, m], yr.at[zz, m], y_dev)

    def s_msg(zz, m):
        ref = place(fam(zz), *s_kind[m])
        return copy(ref, ref, ss.at[zz, m], sr.at[zz, m], sib_dev)

    def s_all(zz):
        ref = hist.at[fam(zz), pl.ds(PAD, 4 * steps)]
        return copy(ref, ref, ss.at[zz, 0], sr.at[zz, 0], sib_dev)

    def s_all_wait(zz):
        ref = hist.at[2 * zz + 1 - core, pl.ds(PAD, 4 * steps)]
        copy(ref, ref, ss.at[zz, 0], sr.at[zz, 0], sib_dev).wait_recv()

    def z_wait(zz, m):
        ref = place(fam(zz), *z_kind[m])
        copy(ref, ref, zs.at[0, zz, m], zr.at[zz, m], x_dev).wait_recv()

    def x_wait(zz, m):
        ref = place(fam(zz), *x_got[m])
        copy(ref, ref, xs.at[zz, m], xr.at[zz, m], x_dev).wait_recv()

    def y_wait(zz, m):
        ref = place(fam(zz), *y_got[m])
        copy(ref, ref, ys.at[zz, m], yr.at[zz, m], y_dev).wait_recv()

    def s_wait(zz, m):
        ref = place(2 * zz + 1 - core, *s_kind[m])
        copy(ref, ref, ss.at[zz, m], sr.at[zz, m], sib_dev).wait_recv()

    can_up, can_down = z < NZ - 1, z > 0

    def own_half(h):
        return new_ref.at[pl.ds(h * half, half)]

    @pl.when(can_up)
    def _():
        z_own(True).start()

    @pl.when(can_down)
    def _():
        z_own(False).start()

    own_x = [copy(own_half(h), place(row, t0, h, half), xs.at[z, h], xr.at[z, h], x_dev)
             for h in (0, 1)]
    own_y = [copy(own_half(1 - m), place(row, t0, 1 - m, half), ys.at[z, m], yr.at[z, m], y_dev)
             for m in (0, 1)]
    for m in (0, 1):
        own_x[m].start()
        own_y[m].start()

    def e_msg(j):
        to = (row + j) % (2 * NZ)
        return copy(ear_ref, ebuf.at[row], es.at[j], er.at[row], {"lag": lag, "row": to})

    def e_wait(j):
        frm = (row + j) % (2 * NZ)
        copy(ear_ref, ebuf.at[frm], es.at[j], er.at[frm], sib_dev).wait_recv()

    for j in range(1, 2 * NZ):
        e_msg(j).start()

    wide_up, wide_down = z < NZ - 2, z > 1
    at_end = (z == 0) | (z == NZ - 1)

    def z_on_both(m):
        @pl.when(wide_up)
        def _():
            z_msg(True, z, m).start()

        @pl.when(wide_down)
        def _():
            z_msg(False, z, m).start()

    def arrive(zz, m, up):
        z_wait(zz, m)

        @pl.when(can_up if up else can_down)
        def _():
            z_msg(up, zz, m).start()

        if m == 0:
            x_msg(zz, 1).start()
            y_msg(zz, 1).start()
        elif m == 1:
            y_msg(zz, 2).start()
        else:
            x_msg(zz, 2).start()

    def rest(zz):
        for m in (1, 2):
            x_wait(zz, m)
            y_wait(zz, m)
        s_all(zz).start()

    def rest_split(zz):
        x_wait(zz, 1)
        s_msg(zz, 1).start()
        y_wait(zz, 1)
        s_msg(zz, 2).start()
        x_wait(zz, 2)
        y_wait(zz, 2)
        s_msg(zz, 3).start()

    wide = 512

    def add_plane(zz, n, first=False):
        total = None
        for c in range(2):
            r = 2 * zz + c
            cols = pl.ds(pl.multiple_of(r * width, width), width)
            term = product(hist[r], mat[n, cols])
            total = term if total is None else total + term
        if first:
            acc[:, n] = total
        else:
            acc[:, n] += total

    def whole(zz):
        s_all_wait(zz)

    def some(zz, i, first=False):
        add_plane(zz, pl.ds(i * wide, wide), first)

    x_wait(z, 0)
    z_on_both(1)
    y_msg(z, 2).start()
    y_wait(z, 0)
    z_on_both(2)
    x_msg(z, 2).start()
    inner = jnp.where(z == 0, 1, NZ - 2)

    @pl.when(at_end)
    def _():
        z_wait(inner, 0)
        for m in (0, 1):
            x_msg(inner, m).start()
            y_msg(inner, m).start()

    @pl.when(jnp.logical_not(at_end))
    def _():
        arrive(z - 1, 0, True)
        arrive(z + 1, 0, False)

    own_copy.wait()
    own_e.wait()
    rest(z)
    @pl.when(at_end)
    def _():
        x_wait(inner, 0)
        y_msg(inner, 2).start()
        y_wait(inner, 0)
        x_msg(inner, 2).start()

    @pl.when(jnp.logical_not(at_end))
    def _():
        for m in (1, 2):
            arrive(z - 1, m, True)
            arrive(z + 1, m, False)

    for j in range(1, 2 * NZ):
        e_wait(j)
    chunk = ear_ref.shape[1]
    for r in range(2 * NZ):
        e = ebuf[r].astype(jnp.float32)
        for j in range(width // chunk):
            cut = 4 * j + 4
            piece = e if cut == PAD else jnp.concatenate([e[cut:], e[:cut]], axis=0)
            hist[r, 0:PAD, j * chunk:(j + 1) * chunk] = piece.astype(hist.dtype)
    mat_copy.wait()
    whole(z)
    for i in range(2):
        some(z, i, first=True)
    low = z < NZ // 2
    last = jnp.where(low, NZ - 1, 0)

    def arrive_far(zz, m, to_sibling=False):
        z_wait(zz, m)
        if m == 0:
            x_msg(zz, 1).start()
            y_msg(zz, 1).start()
            if to_sibling:
                s_msg(zz, 0).start()
        elif m == 1:
            y_msg(zz, 2).start()
        else:
            x_msg(zz, 2).start()

    @pl.when(at_end)
    def _():
        second = jnp.where(low, 2, NZ - 3)
        arrive_far(second, 0)
        rest(inner)
        arrive_far(second, 1)
        arrive_far(second, 2)
        whole(inner)
        for i in range(2):
            some(inner, i)
        arrive_far(last, 0, True)
        rest(second)
        whole(second)
        arrive_far(last, 1)
        arrive_far(last, 2)
        for i in range(2):
            some(second, i)

    @pl.when(jnp.logical_not(at_end))
    def _():
        def on(m):
            z_wait(last, m)

            @pl.when(low)
            def _():
                z_msg(False, last, m).start()

            @pl.when(jnp.logical_not(low))
            def _():
                z_msg(True, last, m).start()

            if m == 0:
                x_msg(last, 1).start()
                y_msg(last, 1).start()
                s_msg(last, 0).start()
            elif m == 1:
                y_msg(last, 2).start()
            else:
                x_msg(last, 2).start()

        on(0)
        rest(z - 1)
        rest(z + 1)
        on(1)
        whole(z - 1)
        some(z - 1, 0)
        on(2)
        some(z - 1, 1)
        whole(z + 1)
        for i in range(2):
            some(z + 1, i)

    rest_split(last)
    for m in range(4):
        s_wait(last, m)

    tile = s_d.shape[2]
    tiles = width // tile

    def shifted(t, h, i):
        start = pl.multiple_of(PAD - 8 + t * steps + h * half, 8)
        part = acc[pl.ds(start, half + 8), i * tile:(i + 1) * tile]
        got = part[8:]
        for k in range(1, 4):
            got = jnp.where(lag == k, part[8 - k:8 - k + half], got)
        return got

    def f_msg(src, dst, h, i, j, dev):
        cut = pl.ds(h * half, half)
        return copy(src.at[i, cut], dst.at[i, cut], fs.at[j, i], fr.at[j, i], dev)

    lo, hi = slice(0, half), slice(half, steps)
    hop_y = [f_msg(s_d, r_d, 0, i, 0, y_dev) for i in range(tiles)]
    hop_x = [f_msg(s_d, r_d, 1, i, 1, x_dev) for i in range(tiles)]
    dir_x = [f_msg(s_x, r_1, 1, i, 2, x_dev) for i in range(tiles)]
    dir_y = [f_msg(s_y, r_1, 0, i, 3, y_dev) for i in range(tiles)]
    last_x = [f_msg(s_x, r_2, 0, i, 4, x_dev) for i in range(tiles)]
    last_y = [f_msg(s_y, r_2, 1, i, 5, y_dev) for i in range(tiles)]
    for i in range(tiles):
        add_plane(last, pl.ds(i * tile, tile))
        s_d[i, lo] = shifted(td, 0, i)
        hop_y[i].start()
        s_d[i, hi] = shifted(td, 1, i)
        hop_x[i].start()
        s_x[i, hi] = shifted(tx, 1, i)
        dir_x[i].start()
        s_y[i, lo] = shifted(ty, 0, i)
        dir_y[i].start()
    for i in range(tiles):
        part_x, part_y = shifted(tx, 0, i), shifted(ty, 1, i)
        hop_y[i].wait_recv()
        s_x[i, lo] = part_x + r_d[i, lo]
        last_x[i].start()
        hop_x[i].wait_recv()
        s_y[i, hi] = part_y + r_d[i, hi]
        last_y[i].start()
    for j in range(1, 2 * NZ):
        e_msg(j).wait_send()
    x_msg(z, 0).wait_send()
    y_msg(z, 0).wait_send()

    @pl.when(at_end)
    def _():
        x_msg(inner, 0).wait_send()
        y_msg(inner, 0).wait_send()

    for zz in range(NZ):
        for m in range(3):
            @pl.when(can_up & (z >= zz) & ((z != zz) | wide_up | (m == 0)))
            def _():
                z_msg(True, zz, m).wait_send()

            @pl.when(can_down & (z <= zz) & ((z != zz) | wide_down | (m == 0)))
            def _():
                z_msg(False, zz, m).wait_send()
        for m in (1, 2):
            x_msg(zz, m).wait_send()
            y_msg(zz, m).wait_send()

        @pl.when(last == zz)
        def _():
            for m in range(4):
                s_msg(zz, m).wait_send()

        @pl.when(last != zz)
        def _():
            s_all(zz).wait_send()
    for i in range(tiles):
        n = slice(i * tile, (i + 1) * tile)
        dir_x[i].wait_recv()
        dir_y[i].wait_recv()
        out_ref[lo, n] = shifted(t0, 0, i) + r_1[i, lo]
        out_ref[hi, n] = shifted(t0, 1, i) + r_1[i, hi]
    for group in (hop_y, hop_x, dir_x, dir_y):
        for c in group:
            c.wait_send()
    for i in range(tiles):
        n = slice(i * tile, (i + 1) * tile)
        last_x[i].wait_recv()
        out_ref[lo, n] += r_2[i, lo]
        last_y[i].wait_recv()
        out_ref[hi, n] += r_2[i, hi]
    for group in (last_x, last_y):
        for c in group:
            c.wait_send()


def on_device(newest, earlier, lag_matrices):
    steps, width = newest.shape
    height = lag_matrices.shape[1]
    count = earlier.shape[0]
    groups = PAD // 4
    packed = jnp.pad(earlier, ((4 - count, 0), (0, 0)))
    packed = packed.reshape(4, groups, width // groups).transpose(1, 0, 2).reshape(PAD, width // groups)
    any_spec = pl.BlockSpec(memory_space=pl.ANY)
    vmem = pl.BlockSpec(memory_space=pltpu.VMEM)
    dma = pltpu.SemaphoreType.DMA
    tile = 256
    block = pltpu.VMEM((height // tile, steps, tile), jnp.float32)
    return pl.pallas_call(
        kernel,
        out_shape=jax.ShapeDtypeStruct((steps, height), jnp.float32),
        in_specs=[any_spec, any_spec, any_spec],
        out_specs=vmem,
        scratch_shapes=[
            pltpu.VMEM((height, 2 * NZ * width), jnp.bfloat16),
            pltpu.VMEM((2 * NZ, PAD + 4 * steps, width), jnp.bfloat16),
            pltpu.VMEM((2 * NZ, PAD, width // groups), jnp.bfloat16),
            pltpu.VMEM((PAD + 4 * steps, height), jnp.float32),
            block, block, block, block, block, block,
            dma((3,)),
            dma((2, NZ, 3)), dma((NZ, 3)),
            dma((NZ, 3)), dma((NZ, 3)),
            dma((NZ, 3)), dma((NZ, 3)),
            dma((NZ, 4)), dma((NZ, 4)),
            dma((2 * NZ,)), dma((2 * NZ,)),
            dma((6, height // tile)), dma((6, height // tile)),
        ],
        compiler_params=pltpu.CompilerParams(
            collective_id=0, has_side_effects=True, vmem_limit_bytes=48 * 1024 * 1024
        ),
        cost_estimate=pl.CostEstimate(
            flops=2 * 4 * steps * height * 2 * NZ * width,
            bytes_accessed=height * 2 * NZ * width * 2, transcendentals=0),
    )(newest, packed, lag_matrices)


def solution(mesh):
    in_specs = (P("lag", "row"), P(None, "row"), P("lag", "row", None))
    out_specs = P("lag", "row")
    fits = mesh.shape["lag"] == 4 and mesh.shape["row"] == 2 * NZ
    return jax.shard_map(
        on_device if fits else on_device_general,
        mesh=mesh, in_specs=in_specs, out_specs=out_specs, check_vma=False
    )
```

```python
import jax
import jax.numpy as jnp
from jax import lax
from jax.experimental import pallas as pl
from jax.experimental.pallas import tpu as pltpu
from jax.sharding import PartitionSpec as P

MESH = pl.DeviceIdType.MESH
PAD = 16
NZ = 4


def product(window, matrix):
    return lax.dot_general(
        window, matrix, (((1,), (1,)), ((), ())), preferred_element_type=jnp.float32
    )


def on_device_general(newest, earlier, lag_matrices):
    lag_index = lax.axis_index("lag")
    matrix = lag_matrices[0]
    own_steps = newest.shape[0]
    earlier_rows = earlier.shape[0]
    wide_newest, wide_earlier = (
        lax.all_gather(newest, "row", axis=1, tiled=True),
        lax.all_gather(earlier, "row", axis=1, tiled=True),
    )
    history = lax.all_gather(wide_newest, "lag", axis=0, tiled=True)
    record = jnp.concatenate([wide_earlier, history], axis=0)
    window = lax.dynamic_slice_in_dim(
        record, jnp.int32(0) + earlier_rows - lag_index, own_steps * lax.axis_size("lag"), 0
    )
    return lax.psum_scatter(product(window, matrix), "lag", scatter_dimension=0, tiled=True)


def kernel(new_ref, ear_ref, mat_ref, out_ref,
           mat, hist, ebuf, acc, s_d, s_x, s_y, r_d, r_1, r_2,
           loc, zs, zr, xs, xr, ys, yr, ss, sr, es, er, fs, fr):
    lag, row = lax.axis_index("lag"), lax.axis_index("row")
    x, y = lag % 2, lag // 2
    z, core = row // 2, row % 2
    sib = row + 1 - 2 * core
    t0, tx, ty = lag, 2 * y + 1 - x, 2 * (1 - y) + x
    td = 2 * (1 - y) + 1 - x
    steps, width = new_ref.shape
    half = steps // 2
    x_dev, y_dev = {"lag": tx, "row": row}, {"lag": ty, "row": row}
    sib_dev = {"lag": lag, "row": sib}

    mat_copy = pltpu.make_async_copy(mat_ref.at[0], mat, loc.at[0])
    mat_copy.start()

    def rows(t, h, n):
        return pl.ds(pl.multiple_of(PAD + t * steps + h * half, 16), n)

    own_copy = pltpu.make_async_copy(new_ref, hist.at[row, rows(t0, 0, steps)], loc.at[1])
    own_copy.start()
    own_e = pltpu.make_async_copy(ear_ref, ebuf.at[row], loc.at[2])
    own_e.start()

    barrier = pltpu.get_barrier_semaphore()
    for dev in (x_dev, y_dev):
        pl.semaphore_signal(barrier, inc=1, device_id=dev, device_id_type=MESH)
    for j in range(1, 2 * NZ):
        pl.semaphore_signal(barrier, inc=1, device_id={"lag": lag, "row": (row + j) % (2 * NZ)},
                            device_id_type=MESH)
    pl.semaphore_wait(barrier, 2 * NZ + 1)

    def copy(src, dst, ssem, rsem, dev):
        return pltpu.make_async_remote_copy(
            src_ref=src, dst_ref=dst, send_sem=ssem, recv_sem=rsem, device_id=dev,
            device_id_type=MESH)

    def place(r, t, h, n):
        return hist.at[r, rows(t, h, n)]

    z_kind = ((t0, 0, steps), (tx, 0, half), (ty, 1, half))
    x_kind = ((t0, 0, half), (t0, 1, half), (ty, 1, half))
    y_kind = ((t0, 1, half), (t0, 0, half), (tx, 0, half))
    s_kind = tuple((t, 0, steps) for t in (t0, tx, ty, td))
    x_got = ((tx, 0, half), (tx, 1, half), (td, 1, half))
    y_got = ((ty, 1, half), (ty, 0, half), (td, 0, half))

    def fam(zz):
        return 2 * zz + core

    def z_msg(up, zz, m):
        dev = {"lag": lag, "row": row + 2 if up else row - 2}
        ref = place(fam(zz), *z_kind[m])
        return copy(ref, ref, zs.at[int(up), zz, m], zr.at[zz, m], dev)

    def z_own(up):
        dev = {"lag": lag, "row": row + 2 if up else row - 2}
        return copy(new_ref, place(row, *z_kind[0]), zs.at[int(up), z, 0], zr.at[z, 0], dev)

    def x_msg(zz, m):
        ref = place(fam(zz), *x_kind[m])
        return copy(ref, ref, xs.at[zz, m], xr.at[zz, m], x_dev)

    def y_msg(zz, m):
        ref = place(fam(zz), *y_kind[m])
        return copy(ref, ref, ys.at[zz, m], yr.at[zz, m], y_dev)

    def s_msg(zz, m):
        ref = place(fam(zz), *s_kind[m])
        return copy(ref, ref, ss.at[zz, m], sr.at[zz, m], sib_dev)

    def z_wait(zz, m):
        ref = place(fam(zz), *z_kind[m])
        copy(ref, ref, zs.at[0, zz, m], zr.at[zz, m], x_dev).wait_recv()

    def x_wait(zz, m):
        ref = place(fam(zz), *x_got[m])
        copy(ref, ref, xs.at[zz, m], xr.at[zz, m], x_dev).wait_recv()

    def y_wait(zz, m):
        ref = place(fam(zz), *y_got[m])
        copy(ref, ref, ys.at[zz, m], yr.at[zz, m], y_dev).wait_recv()

    def s_wait(zz, m):
        ref = place(2 * zz + 1 - core, *s_kind[m])
        copy(ref, ref, ss.at[zz, m], sr.at[zz, m], sib_dev).wait_recv()

    can_up, can_down = z < NZ - 1, z > 0

    def own_half(h):
        return new_ref.at[pl.ds(h * half, half)]

    @pl.when(can_up)
    def _():
        z_own(True).start()

    @pl.when(can_down)
    def _():
        z_own(False).start()

    own_x = [copy(own_half(h), place(row, t0, h, half), xs.at[z, h], xr.at[z, h], x_dev)
             for h in (0, 1)]
    own_y = [copy(own_half(1 - m), place(row, t0, 1 - m, half), ys.at[z, m], yr.at[z, m], y_dev)
             for m in (0, 1)]
    for m in (0, 1):
        own_x[m].start()
        own_y[m].start()
    copy(new_ref, place(row, t0, 0, steps), ss.at[z, 0], sr.at[z, 0], sib_dev).start()

    def e_msg(j):
        to = (row + j) % (2 * NZ)
        return copy(ear_ref, ebuf.at[row], es.at[j], er.at[row], {"lag": lag, "row": to})

    def e_wait(j):
        frm = (row + j) % (2 * NZ)
        copy(ear_ref, ebuf.at[frm], es.at[j], er.at[frm], sib_dev).wait_recv()

    for j in range(1, 2 * NZ):
        e_msg(j).start()

    wide_up, wide_down = z < NZ - 2, z > 1
    at_end = (z == 0) | (z == NZ - 1)

    def z_on_both(m):
        @pl.when(wide_up)
        def _():
            z_msg(True, z, m).start()

        @pl.when(wide_down)
        def _():
            z_msg(False, z, m).start()

    def arrive(zz, m, up):
        z_wait(zz, m)

        @pl.when(can_up if up else can_down)
        def _():
            z_msg(up, zz, m).start()

        if m == 0:
            x_msg(zz, 1).start()
            y_msg(zz, 1).start()
            s_msg(zz, 0).start()
        elif m == 1:
            y_msg(zz, 2).start()
        else:
            x_msg(zz, 2).start()

    def rest(zz):
        x_wait(zz, 1)
        s_msg(zz, 1).start()
        y_wait(zz, 1)
        s_msg(zz, 2).start()
        x_wait(zz, 2)
        y_wait(zz, 2)
        s_msg(zz, 3).start()

    wide = 512

    def add_plane(zz, n, first=False):
        total = None
        for c in range(2):
            r = 2 * zz + c
            cols = pl.ds(pl.multiple_of(r * width, width), width)
            term = product(hist[r], mat[n, cols])
            total = term if total is None else total + term
        if first:
            acc[:, n] = total
        else:
            acc[:, n] += total

    def whole(zz):
        for m in range(4):
            s_wait(zz, m)

    def some(zz, i, first=False):
        add_plane(zz, pl.ds(i * wide, wide), first)

    x_wait(z, 0)
    z_on_both(1)
    y_msg(z, 2).start()
    y_wait(z, 0)
    z_on_both(2)
    x_msg(z, 2).start()
    inner = jnp.where(z == 0, 1, NZ - 2)

    @pl.when(at_end)
    def _():
        z_wait(inner, 0)
        for m in (0, 1):
            x_msg(inner, m).start()
            y_msg(inner, m).start()
        s_msg(inner, 0).start()

    @pl.when(jnp.logical_not(at_end))
    def _():
        arrive(z - 1, 0, True)
        arrive(z + 1, 0, False)

    own_copy.wait()
    own_e.wait()
    rest(z)
    @pl.when(at_end)
    def _():
        x_wait(inner, 0)
        y_msg(inner, 2).start()
        y_wait(inner, 0)
        x_msg(inner, 2).start()

    @pl.when(jnp.logical_not(at_end))
    def _():
        for m in (1, 2):
            arrive(z - 1, m, True)
            arrive(z + 1, m, False)

    for j in range(1, 2 * NZ):
        e_wait(j)
    chunk = ear_ref.shape[1]
    for r in range(2 * NZ):
        e = ebuf[r].astype(jnp.float32)
        for j in range(width // chunk):
            cut = 4 * j + 4
            piece = e if cut == PAD else jnp.concatenate([e[cut:], e[:cut]], axis=0)
            hist[r, 0:PAD, j * chunk:(j + 1) * chunk] = piece.astype(hist.dtype)
    mat_copy.wait()
    whole(z)
    for i in range(2):
        some(z, i, first=True)
    low = z < NZ // 2
    last = jnp.where(low, NZ - 1, 0)

    def arrive_far(zz, m):
        z_wait(zz, m)
        if m == 0:
            x_msg(zz, 1).start()
            y_msg(zz, 1).start()
            s_msg(zz, 0).start()
        elif m == 1:
            y_msg(zz, 2).start()
        else:
            x_msg(zz, 2).start()

    @pl.when(at_end)
    def _():
        second = jnp.where(low, 2, NZ - 3)
        arrive_far(second, 0)
        rest(inner)
        arrive_far(second, 1)
        arrive_far(second, 2)
        whole(inner)
        for i in range(2):
            some(inner, i)
        arrive_far(last, 0)
        rest(second)
        whole(second)
        arrive_far(last, 1)
        arrive_far(last, 2)
        for i in range(2):
            some(second, i)

    @pl.when(jnp.logical_not(at_end))
    def _():
        def on(m):
            z_wait(last, m)

            @pl.when(low)
            def _():
                z_msg(False, last, m).start()

            @pl.when(jnp.logical_not(low))
            def _():
                z_msg(True, last, m).start()

            if m == 0:
                x_msg(last, 1).start()
                y_msg(last, 1).start()
                s_msg(last, 0).start()
            elif m == 1:
                y_msg(last, 2).start()
            else:
                x_msg(last, 2).start()

        on(0)
        rest(z - 1)
        rest(z + 1)
        on(1)
        whole(z - 1)
        some(z - 1, 0)
        on(2)
        some(z - 1, 1)
        whole(z + 1)
        for i in range(2):
            some(z + 1, i)

    rest(last)
    whole(last)

    tile = s_d.shape[2]
    tiles = width // tile

    def shifted(t, h, i):
        start = pl.multiple_of(PAD - 8 + t * steps + h * half, 8)
        part = acc[pl.ds(start, half + 8), i * tile:(i + 1) * tile]
        got = part[8:]
        for k in range(1, 4):
            got = jnp.where(lag == k, part[8 - k:8 - k + half], got)
        return got

    def f_msg(src, dst, h, i, j, dev):
        cut = pl.ds(h * half, half)
        return copy(src.at[i, cut], dst.at[i, cut], fs.at[j, i], fr.at[j, i], dev)

    lo, hi = slice(0, half), slice(half, steps)
    hop_y = [f_msg(s_d, r_d, 0, i, 0, y_dev) for i in range(tiles)]
    hop_x = [f_msg(s_d, r_d, 1, i, 1, x_dev) for i in range(tiles)]
    dir_x = [f_msg(s_x, r_1, 1, i, 2, x_dev) for i in range(tiles)]
    dir_y = [f_msg(s_y, r_1, 0, i, 3, y_dev) for i in range(tiles)]
    last_x = [f_msg(s_x, r_2, 0, i, 4, x_dev) for i in range(tiles)]
    last_y = [f_msg(s_y, r_2, 1, i, 5, y_dev) for i in range(tiles)]
    for i in range(tiles):
        add_plane(last, pl.ds(i * tile, tile))
        s_d[i, lo] = shifted(td, 0, i)
        hop_y[i].start()
        s_d[i, hi] = shifted(td, 1, i)
        hop_x[i].start()
        s_x[i, hi] = shifted(tx, 1, i)
        dir_x[i].start()
        s_y[i, lo] = shifted(ty, 0, i)
        dir_y[i].start()
    for i in range(tiles):
        part_x, part_y = shifted(tx, 0, i), shifted(ty, 1, i)
        hop_y[i].wait_recv()
        s_x[i, lo] = part_x + r_d[i, lo]
        last_x[i].start()
        hop_x[i].wait_recv()
        s_y[i, hi] = part_y + r_d[i, hi]
        last_y[i].start()
    for i in range(tiles):
        n = slice(i * tile, (i + 1) * tile)
        dir_x[i].wait_recv()
        dir_y[i].wait_recv()
        out_ref[lo, n] = shifted(t0, 0, i) + r_1[i, lo]
        out_ref[hi, n] = shifted(t0, 1, i) + r_1[i, hi]
    for i in range(tiles):
        n = slice(i * tile, (i + 1) * tile)
        last_x[i].wait_recv()
        out_ref[lo, n] += r_2[i, lo]
        last_y[i].wait_recv()
        out_ref[hi, n] += r_2[i, hi]

    for group in (hop_y, hop_x, dir_x, dir_y, last_x, last_y):
        for c in group:
            c.wait_send()
    for j in range(1, 2 * NZ):
        e_msg(j).wait_send()
    x_msg(z, 0).wait_send()
    y_msg(z, 0).wait_send()

    @pl.when(at_end)
    def _():
        x_msg(inner, 0).wait_send()
        y_msg(inner, 0).wait_send()

    for zz in range(NZ):
        for m in range(3):
            @pl.when(can_up & (z >= zz) & ((z != zz) | wide_up | (m == 0)))
            def _():
                z_msg(True, zz, m).wait_send()

            @pl.when(can_down & (z <= zz) & ((z != zz) | wide_down | (m == 0)))
            def _():
                z_msg(False, zz, m).wait_send()
        for m in (1, 2):
            x_msg(zz, m).wait_send()
            y_msg(zz, m).wait_send()
        for m in range(4):
            s_msg(zz, m).wait_send()


def on_device(newest, earlier, lag_matrices):
    steps, width = newest.shape
    height = lag_matrices.shape[1]
    count = earlier.shape[0]
    groups = PAD // 4
    packed = jnp.pad(earlier, ((4 - count, 0), (0, 0)))
    packed = packed.reshape(4, groups, width // groups).transpose(1, 0, 2).reshape(PAD, width // groups)
    any_spec = pl.BlockSpec(memory_space=pl.ANY)
    vmem = pl.BlockSpec(memory_space=pltpu.VMEM)
    dma = pltpu.SemaphoreType.DMA
    tile = 512
    block = pltpu.VMEM((height // tile, steps, tile), jnp.float32)
    return pl.pallas_call(
        kernel,
        out_shape=jax.ShapeDtypeStruct((steps, height), jnp.float32),
        in_specs=[any_spec, any_spec, any_spec],
        out_specs=vmem,
        scratch_shapes=[
            pltpu.VMEM((height, 2 * NZ * width), jnp.bfloat16),
            pltpu.VMEM((2 * NZ, PAD + 4 * steps, width), jnp.bfloat16),
            pltpu.VMEM((2 * NZ, PAD, width // groups), jnp.bfloat16),
            pltpu.VMEM((PAD + 4 * steps, height), jnp.float32),
            block, block, block, block, block, block,
            dma((3,)),
            dma((2, NZ, 3)), dma((NZ, 3)),
            dma((NZ, 3)), dma((NZ, 3)),
            dma((NZ, 3)), dma((NZ, 3)),
            dma((NZ, 4)), dma((NZ, 4)),
            dma((2 * NZ,)), dma((2 * NZ,)),
            dma((6, height // tile)), dma((6, height // tile)),
        ],
        compiler_params=pltpu.CompilerParams(
            collective_id=0, has_side_effects=True, vmem_limit_bytes=48 * 1024 * 1024
        ),
        cost_estimate=pl.CostEstimate(
            flops=2 * 4 * steps * height * 2 * NZ * width,
            bytes_accessed=height * 2 * NZ * width * 2, transcendentals=0),
    )(newest, packed, lag_matrices)


def solution(mesh):
    in_specs = (P("lag", "row"), P(None, "row"), P("lag", "row", None))
    out_specs = P("lag", "row")
    fits = mesh.shape["lag"] == 4 and mesh.shape["row"] == 2 * NZ
    return jax.shard_map(
        on_device if fits else on_device_general,
        mesh=mesh, in_specs=in_specs, out_specs=out_specs, check_vma=False
    )
```

```python
import jax
import jax.numpy as jnp
from jax import lax
from jax.experimental import pallas as pl
from jax.experimental.pallas import tpu as pltpu
from jax.sharding import PartitionSpec as P

MESH = pl.DeviceIdType.MESH
PAD = 16
NZ = 4


def product(window, matrix):
    return lax.dot_general(
        window, matrix, (((1,), (1,)), ((), ())), preferred_element_type=jnp.float32
    )


def on_device_general(newest, earlier, lag_matrices):
    lag_index = lax.axis_index("lag")
    matrix = lag_matrices[0]
    own_steps = newest.shape[0]
    earlier_rows = earlier.shape[0]
    wide_newest, wide_earlier = (
        lax.all_gather(newest, "row", axis=1, tiled=True),
        lax.all_gather(earlier, "row", axis=1, tiled=True),
    )
    history = lax.all_gather(wide_newest, "lag", axis=0, tiled=True)
    record = jnp.concatenate([wide_earlier, history], axis=0)
    window = lax.dynamic_slice_in_dim(
        record, jnp.int32(0) + earlier_rows - lag_index, own_steps * lax.axis_size("lag"), 0
    )
    return lax.psum_scatter(product(window, matrix), "lag", scatter_dimension=0, tiled=True)


def kernel(new_ref, ear_ref, mat_ref, out_ref,
           mat, hist, ebuf, acc, s_d, s_x, s_y, r_d, r_1, r_2,
           loc, zs, zr, xs, xr, ys, yr, ss, sr, es, er, fs, fr):
    lag, row = lax.axis_index("lag"), lax.axis_index("row")
    x, y = lag % 2, lag // 2
    z, core = row // 2, row % 2
    sib = row + 1 - 2 * core
    t0, tx, ty = lag, 2 * y + 1 - x, 2 * (1 - y) + x
    td = 2 * (1 - y) + 1 - x
    steps, width = new_ref.shape
    half = steps // 2
    x_dev, y_dev = {"lag": tx, "row": row}, {"lag": ty, "row": row}
    sib_dev = {"lag": lag, "row": sib}

    mat_copy = pltpu.make_async_copy(mat_ref.at[0], mat, loc.at[0])
    mat_copy.start()

    def rows(t, h, n):
        return pl.ds(pl.multiple_of(PAD + t * steps + h * half, 16), n)

    own_copy = pltpu.make_async_copy(new_ref, hist.at[row, rows(t0, 0, steps)], loc.at[1])
    own_copy.start()
    own_e = pltpu.make_async_copy(ear_ref, ebuf.at[row], loc.at[2])
    own_e.start()

    barrier = pltpu.get_barrier_semaphore()
    for dev in (x_dev, y_dev):
        pl.semaphore_signal(barrier, inc=1, device_id=dev, device_id_type=MESH)
    for j in range(1, 2 * NZ):
        pl.semaphore_signal(barrier, inc=1, device_id={"lag": lag, "row": (row + j) % (2 * NZ)},
                            device_id_type=MESH)
    pl.semaphore_wait(barrier, 2 * NZ + 1)

    def copy(src, dst, ssem, rsem, dev):
        return pltpu.make_async_remote_copy(
            src_ref=src, dst_ref=dst, send_sem=ssem, recv_sem=rsem, device_id=dev,
            device_id_type=MESH)

    def place(r, t, h, n):
        return hist.at[r, rows(t, h, n)]

    z_kind = ((t0, 0, steps), (tx, 0, half), (ty, 1, half))
    x_kind = ((t0, 0, half), (t0, 1, half), (ty, 1, half))
    y_kind = ((t0, 1, half), (t0, 0, half), (tx, 0, half))
    s_kind = tuple((t, 0, steps) for t in (t0, tx, ty, td))
    x_got = ((tx, 0, half), (tx, 1, half), (td, 1, half))
    y_got = ((ty, 1, half), (ty, 0, half), (td, 0, half))

    def fam(zz):
        return 2 * zz + core

    def z_msg(up, zz, m):
        dev = {"lag": lag, "row": row + 2 if up else row - 2}
        ref = place(fam(zz), *z_kind[m])
        return copy(ref, ref, zs.at[int(up), zz, m], zr.at[zz, m], dev)

    def z_own(up):
        dev = {"lag": lag, "row": row + 2 if up else row - 2}
        return copy(new_ref, place(row, *z_kind[0]), zs.at[int(up), z, 0], zr.at[z, 0], dev)

    def x_msg(zz, m):
        ref = place(fam(zz), *x_kind[m])
        return copy(ref, ref, xs.at[zz, m], xr.at[zz, m], x_dev)

    def y_msg(zz, m):
        ref = place(fam(zz), *y_kind[m])
        return copy(ref, ref, ys.at[zz, m], yr.at[zz, m], y_dev)

    def s_msg(zz, m):
        ref = place(fam(zz), *s_kind[m])
        return copy(ref, ref, ss.at[zz, m], sr.at[zz, m], sib_dev)

    def z_wait(zz, m):
        ref = place(fam(zz), *z_kind[m])
        copy(ref, ref, zs.at[0, zz, m], zr.at[zz, m], x_dev).wait_recv()

    def x_wait(zz, m):
        ref = place(fam(zz), *x_got[m])
        copy(ref, ref, xs.at[zz, m], xr.at[zz, m], x_dev).wait_recv()

    def y_wait(zz, m):
        ref = place(fam(zz), *y_got[m])
        copy(ref, ref, ys.at[zz, m], yr.at[zz, m], y_dev).wait_recv()

    def s_wait(zz, m):
        ref = place(2 * zz + 1 - core, *s_kind[m])
        copy(ref, ref, ss.at[zz, m], sr.at[zz, m], sib_dev).wait_recv()

    can_up, can_down = z < NZ - 1, z > 0

    def own_half(h):
        return new_ref.at[pl.ds(h * half, half)]

    @pl.when(can_up)
    def _():
        z_own(True).start()

    @pl.when(can_down)
    def _():
        z_own(False).start()

    own_x = [copy(own_half(h), place(row, t0, h, half), xs.at[z, h], xr.at[z, h], x_dev)
             for h in (0, 1)]
    own_y = [copy(own_half(1 - m), place(row, t0, 1 - m, half), ys.at[z, m], yr.at[z, m], y_dev)
             for m in (0, 1)]
    for m in (0, 1):
        own_x[m].start()
        own_y[m].start()
    copy(new_ref, place(row, t0, 0, steps), ss.at[z, 0], sr.at[z, 0], sib_dev).start()

    def e_msg(j):
        to = (row + j) % (2 * NZ)
        return copy(ear_ref, ebuf.at[row], es.at[j], er.at[row], {"lag": lag, "row": to})

    def e_wait(j):
        frm = (row + j) % (2 * NZ)
        copy(ear_ref, ebuf.at[frm], es.at[j], er.at[frm], sib_dev).wait_recv()

    for j in range(1, 2 * NZ):
        e_msg(j).start()

    wide_up, wide_down = z < NZ - 2, z > 1
    at_end = (z == 0) | (z == NZ - 1)

    def z_on_both(m):
        @pl.when(wide_up)
        def _():
            z_msg(True, z, m).start()

        @pl.when(wide_down)
        def _():
            z_msg(False, z, m).start()

    def arrive(zz, m, up):
        z_wait(zz, m)

        @pl.when(can_up if up else can_down)
        def _():
            z_msg(up, zz, m).start()

        if m == 0:
            x_msg(zz, 1).start()
            y_msg(zz, 1).start()
            s_msg(zz, 0).start()
        elif m == 1:
            y_msg(zz, 2).start()
        else:
            x_msg(zz, 2).start()

    def rest(zz):
        x_wait(zz, 1)
        s_msg(zz, 1).start()
        y_wait(zz, 1)
        s_msg(zz, 2).start()
        x_wait(zz, 2)
        y_wait(zz, 2)
        s_msg(zz, 3).start()

    wide = 512

    def add_plane(zz, n, first=False):
        total = None
        for c in range(2):
            r = 2 * zz + c
            cols = pl.ds(pl.multiple_of(r * width, width), width)
            term = product(hist[r], mat[n, cols])
            total = term if total is None else total + term
        if first:
            acc[:, n] = total
        else:
            acc[:, n] += total

    def whole(zz):
        for m in range(4):
            s_wait(zz, m)

    def some(zz, i, first=False):
        add_plane(zz, pl.ds(i * wide, wide), first)

    x_wait(z, 0)
    z_on_both(1)
    y_msg(z, 2).start()
    y_wait(z, 0)
    z_on_both(2)
    x_msg(z, 2).start()
    inner = jnp.where(z == 0, 1, NZ - 2)

    @pl.when(at_end)
    def _():
        z_wait(inner, 0)
        for m in (0, 1):
            x_msg(inner, m).start()
            y_msg(inner, m).start()
        s_msg(inner, 0).start()

    @pl.when(jnp.logical_not(at_end))
    def _():
        arrive(z - 1, 0, True)
        arrive(z + 1, 0, False)

    own_copy.wait()
    own_e.wait()
    rest(z)
    @pl.when(at_end)
    def _():
        x_wait(inner, 0)
        y_msg(inner, 2).start()
        y_wait(inner, 0)
        x_msg(inner, 2).start()

    @pl.when(jnp.logical_not(at_end))
    def _():
        for m in (1, 2):
            arrive(z - 1, m, True)
            arrive(z + 1, m, False)

    for j in range(1, 2 * NZ):
        e_wait(j)
    chunk = ear_ref.shape[1]
    for r in range(2 * NZ):
        e = ebuf[r].astype(jnp.float32)
        for j in range(width // chunk):
            cut = 4 * j + 4
            piece = e if cut == PAD else jnp.concatenate([e[cut:], e[:cut]], axis=0)
            hist[r, 0:PAD, j * chunk:(j + 1) * chunk] = piece.astype(hist.dtype)
    mat_copy.wait()
    whole(z)
    for i in range(2):
        some(z, i, first=True)
    low = z < NZ // 2
    last = jnp.where(low, NZ - 1, 0)

    def arrive_far(zz, m):
        z_wait(zz, m)
        if m == 0:
            x_msg(zz, 1).start()
            y_msg(zz, 1).start()
            s_msg(zz, 0).start()
        elif m == 1:
            y_msg(zz, 2).start()
        else:
            x_msg(zz, 2).start()

    @pl.when(at_end)
    def _():
        second = jnp.where(low, 2, NZ - 3)
        arrive_far(second, 0)
        arrive_far(second, 1)
        arrive_far(second, 2)
        rest(inner)
        whole(inner)
        for i in range(2):
            some(inner, i)
        arrive_far(last, 0)
        rest(second)
        whole(second)
        arrive_far(last, 1)
        arrive_far(last, 2)
        for i in range(2):
            some(second, i)

    @pl.when(jnp.logical_not(at_end))
    def _():
        def on(m):
            z_wait(last, m)

            @pl.when(low)
            def _():
                z_msg(False, last, m).start()

            @pl.when(jnp.logical_not(low))
            def _():
                z_msg(True, last, m).start()

            if m == 0:
                x_msg(last, 1).start()
                y_msg(last, 1).start()
                s_msg(last, 0).start()
            elif m == 1:
                y_msg(last, 2).start()
            else:
                x_msg(last, 2).start()

        on(0)
        rest(z - 1)
        rest(z + 1)
        on(1)
        whole(z - 1)
        some(z - 1, 0)
        on(2)
        some(z - 1, 1)
        whole(z + 1)
        for i in range(2):
            some(z + 1, i)

    rest(last)
    whole(last)

    tile = s_d.shape[2]
    tiles = width // tile

    def shifted(t, h, i):
        start = pl.multiple_of(PAD - 8 + t * steps + h * half, 8)
        part = acc[pl.ds(start, half + 8), i * tile:(i + 1) * tile]
        got = part[8:]
        for k in range(1, 4):
            got = jnp.where(lag == k, part[8 - k:8 - k + half], got)
        return got

    def f_msg(src, dst, h, i, j, dev):
        cut = pl.ds(h * half, half)
        return copy(src.at[i, cut], dst.at[i, cut], fs.at[j, i], fr.at[j, i], dev)

    lo, hi = slice(0, half), slice(half, steps)
    hop_y = [f_msg(s_d, r_d, 0, i, 0, y_dev) for i in range(tiles)]
    hop_x = [f_msg(s_d, r_d, 1, i, 1, x_dev) for i in range(tiles)]
    dir_x = [f_msg(s_x, r_1, 1, i, 2, x_dev) for i in range(tiles)]
    dir_y = [f_msg(s_y, r_1, 0, i, 3, y_dev) for i in range(tiles)]
    last_x = [f_msg(s_x, r_2, 0, i, 4, x_dev) for i in range(tiles)]
    last_y = [f_msg(s_y, r_2, 1, i, 5, y_dev) for i in range(tiles)]
    for i in range(tiles):
        add_plane(last, pl.ds(i * tile, tile))
        s_d[i, lo] = shifted(td, 0, i)
        hop_y[i].start()
        s_d[i, hi] = shifted(td, 1, i)
        hop_x[i].start()
        s_x[i, hi] = shifted(tx, 1, i)
        dir_x[i].start()
        s_y[i, lo] = shifted(ty, 0, i)
        dir_y[i].start()
    for i in range(tiles):
        part_x, part_y = shifted(tx, 0, i), shifted(ty, 1, i)
        hop_y[i].wait_recv()
        s_x[i, lo] = part_x + r_d[i, lo]
        last_x[i].start()
        hop_x[i].wait_recv()
        s_y[i, hi] = part_y + r_d[i, hi]
        last_y[i].start()
    for i in range(tiles):
        n = slice(i * tile, (i + 1) * tile)
        dir_x[i].wait_recv()
        dir_y[i].wait_recv()
        out_ref[lo, n] = shifted(t0, 0, i) + r_1[i, lo]
        out_ref[hi, n] = shifted(t0, 1, i) + r_1[i, hi]
    for i in range(tiles):
        n = slice(i * tile, (i + 1) * tile)
        last_x[i].wait_recv()
        out_ref[lo, n] += r_2[i, lo]
        last_y[i].wait_recv()
        out_ref[hi, n] += r_2[i, hi]

    for group in (hop_y, hop_x, dir_x, dir_y, last_x, last_y):
        for c in group:
            c.wait_send()
    for j in range(1, 2 * NZ):
        e_msg(j).wait_send()
    x_msg(z, 0).wait_send()
    y_msg(z, 0).wait_send()

    @pl.when(at_end)
    def _():
        x_msg(inner, 0).wait_send()
        y_msg(inner, 0).wait_send()

    for zz in range(NZ):
        for m in range(3):
            @pl.when(can_up & (z >= zz) & ((z != zz) | wide_up | (m == 0)))
            def _():
                z_msg(True, zz, m).wait_send()

            @pl.when(can_down & (z <= zz) & ((z != zz) | wide_down | (m == 0)))
            def _():
                z_msg(False, zz, m).wait_send()
        for m in (1, 2):
            x_msg(zz, m).wait_send()
            y_msg(zz, m).wait_send()
        for m in range(4):
            s_msg(zz, m).wait_send()


def on_device(newest, earlier, lag_matrices):
    steps, width = newest.shape
    height = lag_matrices.shape[1]
    count = earlier.shape[0]
    groups = PAD // 4
    packed = jnp.pad(earlier, ((4 - count, 0), (0, 0)))
    packed = packed.reshape(4, groups, width // groups).transpose(1, 0, 2).reshape(PAD, width // groups)
    any_spec = pl.BlockSpec(memory_space=pl.ANY)
    vmem = pl.BlockSpec(memory_space=pltpu.VMEM)
    dma = pltpu.SemaphoreType.DMA
    tile = 512
    block = pltpu.VMEM((height // tile, steps, tile), jnp.float32)
    return pl.pallas_call(
        kernel,
        out_shape=jax.ShapeDtypeStruct((steps, height), jnp.float32),
        in_specs=[any_spec, any_spec, any_spec],
        out_specs=vmem,
        scratch_shapes=[
            pltpu.VMEM((height, 2 * NZ * width), jnp.bfloat16),
            pltpu.VMEM((2 * NZ, PAD + 4 * steps, width), jnp.bfloat16),
            pltpu.VMEM((2 * NZ, PAD, width // groups), jnp.bfloat16),
            pltpu.VMEM((PAD + 4 * steps, height), jnp.float32),
            block, block, block, block, block, block,
            dma((3,)),
            dma((2, NZ, 3)), dma((NZ, 3)),
            dma((NZ, 3)), dma((NZ, 3)),
            dma((NZ, 3)), dma((NZ, 3)),
            dma((NZ, 4)), dma((NZ, 4)),
            dma((2 * NZ,)), dma((2 * NZ,)),
            dma((6, height // tile)), dma((6, height // tile)),
        ],
        compiler_params=pltpu.CompilerParams(
            collective_id=0, has_side_effects=True, vmem_limit_bytes=48 * 1024 * 1024
        ),
        cost_estimate=pl.CostEstimate(
            flops=2 * 4 * steps * height * 2 * NZ * width,
            bytes_accessed=height * 2 * NZ * width * 2, transcendentals=0),
    )(newest, packed, lag_matrices)


def solution(mesh):
    in_specs = (P("lag", "row"), P(None, "row"), P("lag", "row", None))
    out_specs = P("lag", "row")
    fits = mesh.shape["lag"] == 4 and mesh.shape["row"] == 2 * NZ
    return jax.shard_map(
        on_device if fits else on_device_general,
        mesh=mesh, in_specs=in_specs, out_specs=out_specs, check_vma=False
    )
```
